32 devices in a mesh: depth: 8 (over y, x, core), screen: 4 (over z).
Axes of the slice: x: 2, y: 2, z: 4, core: 2. Of those that a mesh axis runs over, the one named last changes fastest.
Arguments:
- density: bfloat16 [80, 384, 2048], P('depth', 'screen'), may hold values from 0.099609375 to 10
- material: int32 [64, 384, 2048], P('depth', 'screen'), may hold values from 0 to 15
- order: int32 [8], replicated, may hold values from 0 to 7, each once
- color_table: float32 [16, 3], replicated, may hold values from 0.3 to 3
- extinction: float32 [16], replicated, may hold values from 0.015625 to 0.15625
Outputs:
- image: float32 [4, 384, 2048], P(None, ('screen', 'depth'))
The draws below stay inside these ranges and needn't reach their ends.
Inputs may be any that keep to these rules, and one draw needn't show every extreme that they name: order is a permutation: each brick has a distinct rank.
All inputs are finite; a program needn't handle non-finite values.
Results may differ from the reference program's by a relative error of at most 0.0003.
Values may be sent and summed in bfloat16 or wider, within the bound.
A program may use at most 128 MiB of HBM per device.

```python
import math
import jax
import jax.numpy as jnp
from jax import lax

NX = 2048
ZB = 8
NTF = 16
BRICKS = 8
NZ = 64
GZ = 80
NY = 384


def set_ends(array, key, low, top_value):
    longest = array.shape.index(max(array.shape))
    spots = []
    for shift in (0, 1):
        where = [jax.random.randint(jax.random.fold_in(key, axis), (), 0, length) for axis, length in enumerate(array.shape)]
        where[longest] = (where[longest] + shift) % array.shape[longest]
        spots.append(tuple(where))
    return array.at[spots[0]].set(low).at[spots[1]].set(top_value)


def block_levels(own_key, dims, shards, smallest, largest):
    loudness, own = 1.0, jax.random.fold_in(own_key, 6)
    for dim, shards_of in shards:
        draws = jnp.exp(jax.random.uniform(jax.random.fold_in(own, dim), (shards_of,), jnp.float32, smallest / len(shards), largest / len(shards)))
        loudness = loudness * jnp.repeat(draws, dims[dim] // shards_of).reshape([-1 if axis == dim else 1 for axis in range(len(dims))])
    return loudness


def setup_inputs(seed: int = 0) -> dict:
    keys = jax.random.split(jax.random.key(seed), 6)
    return {
        "density": jnp.clip(jnp.exp(math.log(10.0) - 4.609084 * jax.random.uniform(keys[0], (GZ, NY, NX), jnp.float32) ** block_levels(keys[0], (GZ, NY, NX), ((0, 8), (1, 4)), -0.2, 0.2)), 0.099609375, 10.0).astype(jnp.bfloat16),
        "material": set_ends(jax.random.randint(keys[1], (NZ, NY, NX), 0, NTF), jax.random.fold_in(keys[1], 1), 0, NTF - 1).astype(jnp.int32),
        "order": jax.random.permutation(keys[2], BRICKS).astype(jnp.int32),
        "color_table": jnp.clip(jnp.exp(jax.random.uniform(keys[3], (NTF, 3), jnp.float32, math.log(0.3), math.log(3.0))), 0.3, 3.0),
        "extinction": jnp.clip(jnp.exp(jax.random.uniform(keys[4], (NTF,), jnp.float32, math.log(0.015625), math.log(0.15625))), 0.015625, 0.15625),
    }


light_x = 0.48
light_y = 0.6
light_z = 0.64

def shade_brick(operands):
    block, kinds, color_table, extinction = operands
    full = block.astype(jnp.float32)
    padded = jnp.pad(full, ((0, 0), (1, 1), (1, 1)))
    grad_z = 0.5 * (full[2:] - full[:-2])
    grad_y = 0.5 * (padded[1:-1, 2:, 1:-1] - padded[1:-1, :-2, 1:-1])
    grad_x = 0.5 * (padded[1:-1, 1:-1, 2:] - padded[1:-1, 1:-1, :-2])
    lit = light_x * grad_x + light_y * grad_y + light_z * grad_z
    shade = 0.55 + 0.45 * lit / jnp.sqrt(1.0 + grad_x * grad_x + grad_y * grad_y + grad_z * grad_z)
    rho = full[1:-1]
    extinct = extinction[kinds] * (rho / (1.0 + rho))
    ahead = jnp.cumsum(extinct, axis=0) - extinct
    weight = jnp.exp(-ahead) * (1.0 - jnp.exp(-extinct)) * shade
    emitted = jnp.stack([lax.optimization_barrier(jnp.sum(weight * color_table[kinds, 0], axis=0)), lax.optimization_barrier(jnp.sum(weight * color_table[kinds, 1], axis=0)), lax.optimization_barrier(jnp.sum(weight * color_table[kinds, 2], axis=0))], axis=0)
    return (emitted, lax.optimization_barrier(jnp.sum(extinct, axis=0)))

def reference(density, material, order, color_table, extinction):
    blocks = density.reshape(BRICKS, ZB + 2, density.shape[1], density.shape[2])
    kinds = material.reshape(BRICKS, ZB, material.shape[1], material.shape[2])
    emitted, optical = lax.map(lambda pair: shade_brick((pair[0], pair[1], color_table, extinction)), (blocks, kinds))
    before = (order[None, :] < order[:, None]).astype(jnp.float32)
    front = jnp.einsum('kj,jyx->kyx', before, optical, precision=lax.Precision.HIGHEST)
    attenuate = jnp.exp(-front)
    colored = jnp.einsum('kcyx,kyx->cyx', emitted, attenuate, precision=lax.Precision.HIGHEST)
    opacity_total = 1.0 - jnp.exp(-lax.optimization_barrier(jnp.sum(optical, axis=0)))
    return jnp.concatenate([colored, opacity_total[None]], axis=0)
```

```python
import functools
import math
import jax
import jax.numpy as jnp
from jax import lax
from jax.experimental import pallas as pl
from jax.experimental.pallas import tpu as pltpu
from jax.sharding import PartitionSpec as P

LIGHT = (0.48, 0.6, 0.64)
MESH = pl.DeviceIdType.MESH
LANES = 128
CODE_TOP = 65000.0
CHUNKS = 2


def kernel(
    bricks, screens, strip,
    dens_hbm, mat_hbm, order_ref, color_ref, ext_ref, out_ref,
    dens, full, mat, sendbuf, recv, halo_out, halo_in,
    dens_sem, mat_sem, halo_send, halo_recv, send_sem, recv_sem, own_sem,
):
    stored, rows, cols = dens.shape
    slices = stored - 2
    unit = math.lcm(8, strip)
    units = rows // unit
    groups = unit // 8
    per_unit = unit // strip
    part = sendbuf.shape[2]
    blocks = strip // part
    entries = ext_ref.shape[0]

    me = lax.axis_index("depth")
    scr = lax.axis_index("screen")
    has_low = scr > 0
    has_high = scr < screens - 1

    own = (me * strip) // unit
    if units == 4:
        visits = [3 - own, own + 1 - 2 * (own % 2), (own + 2) % 4, own]
    else:
        visits = [(own + 1 + j) % units for j in range(units)]

    def dens_copy(h):
        half = rows // 2
        return pltpu.make_async_copy(
            dens_hbm.at[:, pl.ds(h * half, half)],
            dens.at[:, pl.ds(h * half, half)],
            dens_sem.at[h],
        )

    def mat_copy(j):
        where = pl.ds(pl.multiple_of(visits[j] * unit, 8), unit)
        return pltpu.make_async_copy(mat_hbm.at[:, where], mat.at[:, where], mat_sem.at[j])

    for h in range(2):
        dens_copy(h).start()
    for j in range(units):
        mat_copy(j).start()

    barrier = pltpu.get_barrier_semaphore()
    for peer in range(bricks):
        @pl.when(me != peer)
        def _():
            pl.semaphore_signal(barrier, inc=1, device_id=(peer, scr), device_id_type=MESH)

    @pl.when(has_low)
    def _():
        pl.semaphore_signal(barrier, inc=1, device_id=(me, scr - 1), device_id_type=MESH)

    @pl.when(has_high)
    def _():
        pl.semaphore_signal(barrier, inc=1, device_id=(me, scr + 1), device_id_type=MESH)

    lane = lax.broadcasted_iota(jnp.int32, (8, LANES), 1)
    sub = lax.broadcasted_iota(jnp.int32, (8, LANES), 0)

    def table(read):
        out = jnp.zeros((8, LANES), jnp.float32)
        for e in range(entries):
            out = jnp.where(lane == e, read(e), out)
        return out

    tabs = [table(lambda e, c=c: color_ref[c, e]) for c in range(3)]
    ext2 = table(lambda e: ext_ref[e]) * math.log2(math.e)
    tops = [jnp.max(t, axis=1, keepdims=True) for t in tabs]
    top_tau = slices * jnp.max(ext2, axis=1, keepdims=True)
    steps = [jnp.broadcast_to(t * (1.0 / CODE_TOP), (8, LANES)) for t in tops + [top_tau]]
    scales = [1.0 / s for s in steps]

    for h in range(2):
        dens_copy(h).wait()

    for z in range(slices):
        halo_out[0, z : z + 1, :] = dens[z + 1, 0:16, :].astype(jnp.float32)[0:1]
        halo_out[1, z : z + 1, :] = dens[z + 1, rows - 16 : rows, :].astype(jnp.float32)[15:16]

    pl.semaphore_wait(
        barrier, bricks - 1 + jnp.where(has_low, 1, 0) + jnp.where(has_high, 1, 0)
    )

    def halo_copy(side):
        return pltpu.make_async_remote_copy(
            src_ref=halo_out.at[side],
            dst_ref=halo_in.at[1 - side],
            send_sem=halo_send.at[side],
            recv_sem=halo_recv.at[1 - side],
            device_id=(me, scr + 2 * side - 1),
            device_id_type=MESH,
        )

    def halo_wait(side):
        pltpu.make_async_remote_copy(
            src_ref=halo_out.at[side],
            dst_ref=halo_in.at[side],
            send_sem=halo_send.at[side],
            recv_sem=halo_recv.at[side],
            device_id=(me, scr + 2 * side - 1),
            device_id_type=MESH,
        ).wait_recv()

    @pl.when(has_low)
    def _():
        halo_copy(0).start()

    @pl.when(has_high)
    def _():
        halo_copy(1).start()

    @pl.loop(0, stored)
    def _(z):
        full[z, 8 : 8 + rows, 0:LANES] = jnp.zeros((rows, LANES), jnp.float32)
        full[z, 8 : 8 + rows, LANES + cols :] = jnp.zeros((rows, LANES), jnp.float32)

        @pl.loop(0, rows // 16)
        def _(i):
            r = pl.multiple_of(i * 16, 16)
            full[z, pl.ds(pl.multiple_of(r + 8, 8), 16), LANES : LANES + cols] = dens[
                z, pl.ds(r, 16), :
            ].astype(jnp.float32)

    def pixel_tile(r, c):
        def tile(z, dr, dc):
            return full[
                z,
                pl.ds(pl.multiple_of(r + 8 + dr * 8, 8), 8),
                pl.ds(pl.multiple_of(c + (1 + dc) * LANES, LANES), LANES),
            ]

        through = jnp.ones((8, LANES), jnp.float32)
        tau = jnp.zeros((8, LANES), jnp.float32)
        sums = [jnp.zeros((8, LANES), jnp.float32) for _ in range(3)]
        before, here = tile(0, 0, 0), tile(1, 0, 0)
        for z in range(slices):
            after = tile(z + 2, 0, 0)
            left = pltpu.roll(jnp.where(lane == LANES - 1, tile(z + 1, 0, -1), here), 1, 1)
            right = pltpu.roll(jnp.where(lane == 0, tile(z + 1, 0, 1), here), LANES - 1, 1)
            up = pltpu.roll(jnp.where(sub == 7, tile(z + 1, -1, 0), here), 1, 0)
            down = pltpu.roll(jnp.where(sub == 0, tile(z + 1, 1, 0), here), 7, 0)
            dx, dy, dz = right - left, down - up, after - before
            square = (dx * dx + dy * dy) + (dz * dz + 4.0)
            lit = (0.45 * LIGHT[0]) * dx + (0.45 * LIGHT[1]) * dy + (0.45 * LIGHT[2]) * dz
            shade = 0.55 + lit * lax.rsqrt(square)
            kinds = mat[z, pl.ds(r, 8), pl.ds(c, LANES)]

            def pick(values):
                return jnp.take_along_axis(values, kinds, axis=1, mode="promise_in_bounds")

            sigma = pick(ext2) * (here / (1.0 + here))
            later = through * jnp.exp2(-sigma)
            weight = (through - later) * shade
            for k in range(3):
                sums[k] = sums[k] + weight * pick(tabs[k])
            tau = tau + sigma
            through = later
            before, here = here, after
        gain = 1.0 / (1.0 - through)
        values = [s * gain for s in sums] + [tau]
        codes = [
            jnp.minimum(v * s + 0.5, 65535.0).astype(jnp.int32) for v, s in zip(values, scales)
        ]
        return [(codes[0] << 16) | codes[1], (codes[2] << 16) | codes[3]]

    def row_group(unit_at, g):
        r = pl.multiple_of(unit_at * unit + g * 8, 8)

        @pl.loop(0, cols // (LANES * CHUNKS))
        def _(i):
            for k in range(CHUNKS):
                c = pl.multiple_of(i * (LANES * CHUNKS) + k * LANES, LANES)
                words = pixel_tile(r, c)
                for p in range(2):
                    for h in range(8 // part):
                        sendbuf[
                            unit_at * (unit // part) + g * (8 // part) + h, p, :, pl.ds(c, LANES)
                        ] = words[p][h * part : (h + 1) * part]

    def strip_copy(s):
        return pltpu.make_async_remote_copy(
            src_ref=sendbuf.at[pl.ds(s * blocks, blocks)],
            dst_ref=recv.at[me],
            send_sem=send_sem.at[s],
            recv_sem=recv_sem.at[me],
            device_id=(s, scr),
            device_id_type=MESH,
        )

    def own_copy():
        return pltpu.make_async_copy(
            sendbuf.at[pl.ds(me * blocks, blocks)], recv.at[me], own_sem
        )

    def set_halo(side, there):
        row = 7 if side == 0 else 8 + rows

        @pl.when(there)
        def _():
            halo_wait(side)
            for z in range(slices):
                full[z + 1, row : row + 1, LANES : LANES + cols] = halo_in[side, z : z + 1, :]

        @pl.when(jnp.logical_not(there))
        def _():
            for z in range(slices):
                full[z + 1, row : row + 1, LANES : LANES + cols] = jnp.zeros(
                    (1, cols), jnp.float32
                )

    for j in range(units):
        at = visits[j]
        mat_copy(j).wait()

        @pl.loop(0, groups)
        def _(i):
            @pl.when(jnp.logical_and(i == groups - 1, at == 0))
            def _():
                set_halo(0, has_low)

            @pl.when(jnp.logical_and(i == groups - 1, at == units - 1))
            def _():
                set_halo(1, has_high)

            row_group(at, jnp.where(at == 0, groups - 1 - i, i))

        for k in range(per_unit):
            s = at * per_unit + k
            if j < units - 1:
                strip_copy(s).start()
            else:
                @pl.when(s != me)
                def _():
                    strip_copy(s).start()

                @pl.when(s == me)
                def _():
                    own_copy().start()

    def brick_at(rank):
        def step(j, found):
            return jnp.maximum(found, jnp.where(order_ref[j] == rank, j, 0))

        return lax.fori_loop(0, bricks, step, jnp.int32(0), unroll=bricks <= 8)

    at_rank = [brick_at(i) for i in range(bricks)]

    own_copy().wait()
    for peer in range(bricks):
        @pl.when(me != peer)
        def _():
            pltpu.make_async_remote_copy(
                src_ref=sendbuf.at[pl.ds(peer * blocks, blocks)],
                dst_ref=recv.at[peer],
                send_sem=send_sem.at[peer],
                recv_sem=recv_sem.at[peer],
                device_id=(peer, scr),
                device_id_type=MESH,
            ).wait_recv()

    width = 4 * LANES
    unscale = [jnp.concatenate([s[:part]] * (width // LANES), axis=1) for s in steps]
    for b in range(blocks):
        @pl.loop(0, cols // width)
        def _(i):
            where = pl.ds(pl.multiple_of(i * width, width), width)
            through = jnp.ones((part, width), jnp.float32)
            sums = [jnp.zeros((part, width), jnp.float32) for _ in range(3)]
            for rank in range(bricks):
                first = recv[at_rank[rank], b, 0, :, where]
                second = recv[at_rank[rank], b, 1, :, where]
                codes = []
                for word in (first, second):
                    codes += [lax.shift_right_logical(word, 16), word & 0xFFFF]
                values = [k.astype(jnp.float32) * s for k, s in zip(codes, unscale)]
                later = through * jnp.exp2(-values[3])
                weight = through - later
                sums = [a + weight * v for a, v in zip(sums, values[:3])]
                through = later
            for k, value in enumerate(sums + [1.0 - through]):
                out_ref[k, b * part : (b + 1) * part, where] = value

    for peer in range(bricks):
        @pl.when(me != peer)
        def _():
            strip_copy(peer).wait_send()

    @pl.when(has_low)
    def _():
        halo_copy(0).wait_send()

    @pl.when(has_high)
    def _():
        halo_copy(1).wait_send()


def solution(mesh):
    bricks, screens = mesh.shape["depth"], mesh.shape["screen"]

    def body(density, material, order, color_table, extinction):
        stored, rows, cols = density.shape
        slices = stored - 2
        strip = rows // bricks
        part = math.gcd(8, strip)
        blocks = strip // part
        smem = pl.BlockSpec(memory_space=pltpu.SMEM)
        hbm = pl.BlockSpec(memory_space=pl.ANY)
        voxels = slices * rows * cols
        return pl.pallas_call(
            functools.partial(kernel, bricks, screens, strip),
            out_shape=jax.ShapeDtypeStruct((4, strip, cols), jnp.float32),
            in_specs=[hbm, hbm, smem, smem, smem],
            out_specs=pl.BlockSpec(memory_space=pltpu.VMEM),
            scratch_shapes=[
                pltpu.VMEM((stored, rows, cols), jnp.bfloat16),
                pltpu.VMEM((stored, rows + 16, cols + 2 * LANES), jnp.float32),
                pltpu.VMEM((slices, rows, cols), jnp.int32),
                pltpu.VMEM((rows // part, 2, part, cols), jnp.int32),
                pltpu.VMEM((bricks, blocks, 2, part, cols), jnp.int32),
                pltpu.VMEM((2, slices, cols), jnp.float32),
                pltpu.VMEM((2, slices, cols), jnp.float32),
                pltpu.SemaphoreType.DMA((2,)),
                pltpu.SemaphoreType.DMA((rows // math.lcm(8, strip),)),
                pltpu.SemaphoreType.DMA((2,)),
                pltpu.SemaphoreType.DMA((2,)),
                pltpu.SemaphoreType.DMA((bricks,)),
                pltpu.SemaphoreType.DMA((bricks,)),
                pltpu.SemaphoreType.DMA,
            ],
            compiler_params=pltpu.CompilerParams(
                collective_id=0, has_side_effects=True, vmem_limit_bytes=48 * 1024 * 1024
            ),
            cost_estimate=pl.CostEstimate(
                flops=60 * voxels, bytes_accessed=7 * voxels, transcendentals=3 * voxels
            ),
        )(density, material, order, color_table.T, extinction)

    placed = (P("depth", "screen", None), P("depth", "screen", None), P(), P(), P())
    return jax.shard_map(
        body,
        mesh=mesh,
        in_specs=placed,
        out_specs=P(None, ("screen", "depth"), None),
        check_vma=False,
    )
```

```python
import functools
import math
import jax
import jax.numpy as jnp
from jax import lax
from jax.experimental import pallas as pl
from jax.experimental.pallas import tpu as pltpu
from jax.sharding import PartitionSpec as P

LIGHT = (0.48, 0.6, 0.64)
MESH = pl.DeviceIdType.MESH
LANES = 128
CODE_TOP = 65000.0
CHUNKS = 4


def kernel(
    bricks, screens, strip,
    dens_hbm, mat_hbm, order_hbm, color_hbm, ext_hbm, out_ref,
    dens, full, mat, sendbuf, recv, halo_out, halo_in,
    dens_sem, mat_sem, halo_send, halo_recv, send_sem, recv_sem, own_sem,
    order_ref, color_ref, ext_ref, small_sem,
):
    stored, rows, cols = dens.shape
    slices = stored - 2
    unit = math.lcm(8, strip)
    units = rows // unit
    groups = unit // 8
    per_unit = unit // strip
    part = sendbuf.shape[2]
    blocks = strip // part
    entries = ext_ref.shape[0]

    me = lax.axis_index("depth")
    scr = lax.axis_index("screen")
    has_low = scr > 0
    has_high = scr < screens - 1

    own = (me * strip) // unit
    if units == 4:
        visits = [3 - own, own + 1 - 2 * (own % 2), (own + 2) % 4, own]
    else:
        visits = [(own + 1 + j) % units for j in range(units)]

    def dens_copy(h):
        half = rows // 2
        return pltpu.make_async_copy(
            dens_hbm.at[:, pl.ds(h * half, half)],
            dens.at[:, pl.ds(h * half, half)],
            dens_sem.at[h],
        )

    def mat_copy(j):
        where = pl.ds(pl.multiple_of(visits[j] * unit, 8), unit)
        return pltpu.make_async_copy(mat_hbm.at[:, where], mat.at[:, where], mat_sem.at[j])

    small = [
        pltpu.make_async_copy(src, dst, small_sem.at[i])
        for i, (src, dst) in enumerate(
            [(order_hbm, order_ref), (color_hbm, color_ref), (ext_hbm, ext_ref)]
        )
    ]
    for copy in small:
        copy.start()
    for h in range(2):
        dens_copy(h).start()
    for j in range(units):
        mat_copy(j).start()

    barrier = pltpu.get_barrier_semaphore()
    for peer in range(bricks):
        @pl.when(me != peer)
        def _():
            pl.semaphore_signal(barrier, inc=1, device_id=(peer, scr), device_id_type=MESH)

    @pl.when(has_low)
    def _():
        pl.semaphore_signal(barrier, inc=1, device_id=(me, scr - 1), device_id_type=MESH)

    @pl.when(has_high)
    def _():
        pl.semaphore_signal(barrier, inc=1, device_id=(me, scr + 1), device_id_type=MESH)

    for copy in small:
        copy.wait()

    lane = lax.broadcasted_iota(jnp.int32, (8, LANES), 1)
    sub = lax.broadcasted_iota(jnp.int32, (8, LANES), 0)

    def table(read):
        out = jnp.zeros((8, LANES), jnp.float32)
        for e in range(entries):
            out = jnp.where(lane == e, read(e), out)
        return out

    tabs = [table(lambda e, c=c: color_ref[c, e]) for c in range(3)]
    ext2 = table(lambda e: ext_ref[e]) * math.log2(math.e)
    tops = [jnp.max(t, axis=1, keepdims=True) for t in tabs]
    top_tau = slices * jnp.max(ext2, axis=1, keepdims=True)
    steps = [jnp.broadcast_to(t * (1.0 / CODE_TOP), (8, LANES)) for t in tops + [top_tau]]
    scales = [1.0 / s for s in steps]

    for h in range(2):
        dens_copy(h).wait()

    for z in range(slices):
        halo_out[0, z : z + 1, :] = dens[z + 1, 0:16, :].astype(jnp.float32)[0:1]
        halo_out[1, z : z + 1, :] = dens[z + 1, rows - 16 : rows, :].astype(jnp.float32)[15:16]

    @pl.loop(0, stored)
    def _(z):
        full[z, 8 : 8 + rows, 0:LANES] = jnp.zeros((rows, LANES), jnp.float32)
        full[z, 8 : 8 + rows, LANES + cols :] = jnp.zeros((rows, LANES), jnp.float32)

        @pl.loop(0, rows // 16)
        def _(i):
            r = pl.multiple_of(i * 16, 16)
            full[z, pl.ds(pl.multiple_of(r + 8, 8), 16), LANES : LANES + cols] = dens[
                z, pl.ds(r, 16), :
            ].astype(jnp.float32)

    pl.semaphore_wait(
        barrier, bricks - 1 + jnp.where(has_low, 1, 0) + jnp.where(has_high, 1, 0)
    )

    def halo_copy(side):
        return pltpu.make_async_remote_copy(
            src_ref=halo_out.at[side],
            dst_ref=halo_in.at[1 - side],
            send_sem=halo_send.at[side],
            recv_sem=halo_recv.at[1 - side],
            device_id=(me, scr + 2 * side - 1),
            device_id_type=MESH,
        )

    def halo_wait(side):
        pltpu.make_async_remote_copy(
            src_ref=halo_out.at[side],
            dst_ref=halo_in.at[side],
            send_sem=halo_send.at[side],
            recv_sem=halo_recv.at[side],
            device_id=(me, scr + 2 * side - 1),
            device_id_type=MESH,
        ).wait_recv()

    @pl.when(has_low)
    def _():
        halo_copy(0).start()

    @pl.when(has_high)
    def _():
        halo_copy(1).start()

    def pixel_tile(r, c):
        def tile(z, dr, dc):
            return full[
                z,
                pl.ds(pl.multiple_of(r + 8 + dr * 8, 8), 8),
                pl.ds(pl.multiple_of(c + (1 + dc) * LANES, LANES), LANES),
            ]

        through = jnp.ones((8, LANES), jnp.float32)
        tau = jnp.zeros((8, LANES), jnp.float32)
        sums = [jnp.zeros((8, LANES), jnp.float32) for _ in range(3)]
        before, here = tile(0, 0, 0), tile(1, 0, 0)
        for z in range(slices):
            after = tile(z + 2, 0, 0)
            left = pltpu.roll(jnp.where(lane == LANES - 1, tile(z + 1, 0, -1), here), 1, 1)
            right = pltpu.roll(jnp.where(lane == 0, tile(z + 1, 0, 1), here), LANES - 1, 1)
            up = pltpu.roll(jnp.where(sub == 7, tile(z + 1, -1, 0), here), 1, 0)
            down = pltpu.roll(jnp.where(sub == 0, tile(z + 1, 1, 0), here), 7, 0)
            dx, dy, dz = right - left, down - up, after - before
            square = (dx * dx + dy * dy) + (dz * dz + 4.0)
            lit = (0.45 * LIGHT[0]) * dx + (0.45 * LIGHT[1]) * dy + (0.45 * LIGHT[2]) * dz
            shade = 0.55 + lit * lax.rsqrt(square)
            kinds = mat[z, pl.ds(r, 8), pl.ds(c, LANES)]

            def pick(values):
                return jnp.take_along_axis(values, kinds, axis=1, mode="promise_in_bounds")

            sigma = pick(ext2) * (here / (1.0 + here))
            later = through * jnp.exp2(-sigma)
            weight = (through - later) * shade
            for k in range(3):
                sums[k] = sums[k] + weight * pick(tabs[k])
            tau = tau + sigma
            through = later
            before, here = here, after
        gain = 1.0 / (1.0 - through)
        values = [s * gain for s in sums] + [tau]
        codes = [
            jnp.minimum(v * s + 0.5, 65535.0).astype(jnp.int32) for v, s in zip(values, scales)
        ]
        return [(codes[0] << 16) | codes[1], (codes[2] << 16) | codes[3]]

    def row_group(unit_at, g):
        r = pl.multiple_of(unit_at * unit + g * 8, 8)

        @pl.loop(0, cols // (LANES * CHUNKS))
        def _(i):
            for k in range(CHUNKS):
                c = pl.multiple_of(i * (LANES * CHUNKS) + k * LANES, LANES)
                words = pixel_tile(r, c)
                for p in range(2):
                    for h in range(8 // part):
                        sendbuf[
                            unit_at * (unit // part) + g * (8 // part) + h, p, :, pl.ds(c, LANES)
                        ] = words[p][h * part : (h + 1) * part]

    def strip_copy(s):
        return pltpu.make_async_remote_copy(
            src_ref=sendbuf.at[pl.ds(s * blocks, blocks)],
            dst_ref=recv.at[me],
            send_sem=send_sem.at[s],
            recv_sem=recv_sem.at[me],
            device_id=(s, scr),
            device_id_type=MESH,
        )

    def own_copy():
        return pltpu.make_async_copy(
            sendbuf.at[pl.ds(me * blocks, blocks)], recv.at[me], own_sem
        )

    def set_halo(side, there):
        row = 7 if side == 0 else 8 + rows

        @pl.when(there)
        def _():
            halo_wait(side)
            for z in range(slices):
                full[z + 1, row : row + 1, LANES : LANES + cols] = halo_in[side, z : z + 1, :]

        @pl.when(jnp.logical_not(there))
        def _():
            for z in range(slices):
                full[z + 1, row : row + 1, LANES : LANES + cols] = jnp.zeros(
                    (1, cols), jnp.float32
                )

    for j in range(units):
        at = visits[j]
        mat_copy(j).wait()

        @pl.loop(0, groups)
        def _(i):
            @pl.when(jnp.logical_and(i == groups - 1, at == 0))
            def _():
                set_halo(0, has_low)

            @pl.when(jnp.logical_and(i == groups - 1, at == units - 1))
            def _():
                set_halo(1, has_high)

            row_group(at, jnp.where(at == 0, groups - 1 - i, i))

        for k in range(per_unit):
            s = at * per_unit + k
            if j < units - 1:
                strip_copy(s).start()
            else:
                @pl.when(s != me)
                def _():
                    strip_copy(s).start()

                @pl.when(s == me)
                def _():
                    own_copy().start()

    def brick_at(rank):
        def step(j, found):
            return jnp.maximum(found, jnp.where(order_ref[j] == rank, j, 0))

        return lax.fori_loop(0, bricks, step, jnp.int32(0), unroll=bricks <= 8)

    at_rank = [brick_at(i) for i in range(bricks)]

    own_copy().wait()
    for peer in range(bricks):
        @pl.when(me != peer)
        def _():
            pltpu.make_async_remote_copy(
                src_ref=sendbuf.at[pl.ds(peer * blocks, blocks)],
                dst_ref=recv.at[peer],
                send_sem=send_sem.at[peer],
                recv_sem=recv_sem.at[peer],
                device_id=(peer, scr),
                device_id_type=MESH,
            ).wait_recv()

    width = 4 * LANES
    unscale = [jnp.concatenate([s[:part]] * (width // LANES), axis=1) for s in steps]
    for b in range(blocks):
        @pl.loop(0, cols // width)
        def _(i):
            where = pl.ds(pl.multiple_of(i * width, width), width)
            through = jnp.ones((part, width), jnp.float32)
            sums = [jnp.zeros((part, width), jnp.float32) for _ in range(3)]
            for rank in range(bricks):
                first = recv[at_rank[rank], b, 0, :, where]
                second = recv[at_rank[rank], b, 1, :, where]
                codes = []
                for word in (first, second):
                    codes += [lax.shift_right_logical(word, 16), word & 0xFFFF]
                values = [k.astype(jnp.float32) * s for k, s in zip(codes, unscale)]
                later = through * jnp.exp2(-values[3])
                weight = through - later
                sums = [a + weight * v for a, v in zip(sums, values[:3])]
                through = later
            for k, value in enumerate(sums + [1.0 - through]):
                out_ref[k, b * part : (b + 1) * part, where] = value

    for peer in range(bricks):
        @pl.when(me != peer)
        def _():
            strip_copy(peer).wait_send()

    @pl.when(has_low)
    def _():
        halo_copy(0).wait_send()

    @pl.when(has_high)
    def _():
        halo_copy(1).wait_send()


def solution(mesh):
    bricks, screens = mesh.shape["depth"], mesh.shape["screen"]

    def body(density, material, order, color_table, extinction):
        stored, rows, cols = density.shape
        slices = stored - 2
        strip = rows // bricks
        part = math.gcd(8, strip)
        blocks = strip // part
        hbm = pl.BlockSpec(memory_space=pl.ANY)
        voxels = slices * rows * cols
        return pl.pallas_call(
            functools.partial(kernel, bricks, screens, strip),
            out_shape=jax.ShapeDtypeStruct((4, strip, cols), jnp.float32),
            in_specs=[hbm] * 5,
            out_specs=pl.BlockSpec(memory_space=pltpu.VMEM),
            scratch_shapes=[
                pltpu.VMEM((stored, rows, cols), jnp.bfloat16),
                pltpu.VMEM((stored, rows + 16, cols + 2 * LANES), jnp.float32),
                pltpu.VMEM((slices, rows, cols), jnp.int32),
                pltpu.VMEM((rows // part, 2, part, cols), jnp.int32),
                pltpu.VMEM((bricks, blocks, 2, part, cols), jnp.int32),
                pltpu.VMEM((2, slices, cols), jnp.float32),
                pltpu.VMEM((2, slices, cols), jnp.float32),
                pltpu.SemaphoreType.DMA((2,)),
                pltpu.SemaphoreType.DMA((rows // math.lcm(8, strip),)),
                pltpu.SemaphoreType.DMA((2,)),
                pltpu.SemaphoreType.DMA((2,)),
                pltpu.SemaphoreType.DMA((bricks,)),
                pltpu.SemaphoreType.DMA((bricks,)),
                pltpu.SemaphoreType.DMA,
                pltpu.SMEM((bricks,), jnp.int32),
                pltpu.SMEM(color_table.shape[::-1], jnp.float32),
                pltpu.SMEM(extinction.shape, jnp.float32),
                pltpu.SemaphoreType.DMA((3,)),
            ],
            compiler_params=pltpu.CompilerParams(
                collective_id=0, has_side_effects=True, vmem_limit_bytes=64 * 1024 * 1024
            ),
            cost_estimate=pl.CostEstimate(
                flops=60 * voxels, bytes_accessed=7 * voxels, transcendentals=3 * voxels
            ),
        )(density, material, order, color_table.T, extinction)

    placed = (P("depth", "screen", None), P("depth", "screen", None), P(), P(), P())
    return jax.shard_map(
        body,
        mesh=mesh,
        in_specs=placed,
        out_specs=P(None, ("screen", "depth"), None),
        check_vma=False,
    )
```

```python
import functools
import math
import jax
import jax.numpy as jnp
from jax import lax
from jax.experimental import pallas as pl
from jax.experimental.pallas import tpu as pltpu
from jax.sharding import PartitionSpec as P

LIGHT = (0.48, 0.6, 0.64)
MESH = pl.DeviceIdType.MESH
LANES = 128
CODE_TOP = 65000.0
CHUNKS = 4


def kernel(
    bricks, screens, strip,
    dens_hbm, mat_hbm, order_hbm, color_hbm, ext_hbm, out_ref,
    dens, full, mat, sendbuf, recv, halo_out, halo_in,
    dens_sem, mat_sem, halo_send, halo_recv, send_sem, recv_sem, own_sem,
    order_ref, color_ref, ext_ref, small_sem,
):
    stored, rows, cols = dens.shape
    slices = stored - 2
    unit = math.lcm(8, strip)
    units = rows // unit
    groups = unit // 8
    per_unit = unit // strip
    part = sendbuf.shape[2]
    blocks = strip // part
    entries = ext_ref.shape[0]

    me = lax.axis_index("depth")
    scr = lax.axis_index("screen")
    has_low = scr > 0
    has_high = scr < screens - 1

    own = (me * strip) // unit
    if units == 4:
        visits = [3 - own, own + 1 - 2 * (own % 2), (own + 2) % 4, own]
    else:
        visits = [(own + 1 + j) % units for j in range(units)]

    def dens_copy(h):
        half = rows // 2
        return pltpu.make_async_copy(
            dens_hbm.at[:, pl.ds(h * half, half)],
            dens.at[:, pl.ds(h * half, half)],
            dens_sem.at[h],
        )

    def mat_copy(j):
        where = pl.ds(pl.multiple_of(visits[j] * unit, 8), unit)
        return pltpu.make_async_copy(mat_hbm.at[:, where], mat.at[:, where], mat_sem.at[j])

    small = [
        pltpu.make_async_copy(src, dst, small_sem.at[i])
        for i, (src, dst) in enumerate(
            [(order_hbm, order_ref), (color_hbm, color_ref), (ext_hbm, ext_ref)]
        )
    ]
    for copy in small:
        copy.start()
    for h in range(2):
        dens_copy(h).start()
    for j in range(units):
        mat_copy(j).start()

    barrier = pltpu.get_barrier_semaphore()
    for peer in range(bricks):
        @pl.when(me != peer)
        def _():
            pl.semaphore_signal(barrier, inc=1, device_id=(peer, scr), device_id_type=MESH)

    @pl.when(has_low)
    def _():
        pl.semaphore_signal(barrier, inc=1, device_id=(me, scr - 1), device_id_type=MESH)

    @pl.when(has_high)
    def _():
        pl.semaphore_signal(barrier, inc=1, device_id=(me, scr + 1), device_id_type=MESH)

    for copy in small:
        copy.wait()

    lane = lax.broadcasted_iota(jnp.int32, (8, LANES), 1)
    sub = lax.broadcasted_iota(jnp.int32, (8, LANES), 0)

    def table(read):
        out = jnp.zeros((8, LANES), jnp.float32)
        for e in range(entries):
            out = jnp.where(lane == e, read(e), out)
        return out

    tabs = [table(lambda e, c=c: color_ref[c, e]) for c in range(3)]
    ext2 = table(lambda e: ext_ref[e]) * math.log2(math.e)
    tops = [jnp.max(t, axis=1, keepdims=True) for t in tabs]
    top_tau = slices * jnp.max(ext2, axis=1, keepdims=True)
    steps = [jnp.broadcast_to(t * (1.0 / CODE_TOP), (8, LANES)) for t in tops + [top_tau]]
    scales = [1.0 / s for s in steps]

    for h in range(2):
        dens_copy(h).wait()

    for z in range(slices):
        halo_out[0, z : z + 1, :] = dens[z + 1, 0:16, :].astype(jnp.float32)[0:1]
        halo_out[1, z : z + 1, :] = dens[z + 1, rows - 16 : rows, :].astype(jnp.float32)[15:16]

    @pl.loop(0, stored)
    def _(z):
        full[z, 8 : 8 + rows, 0:LANES] = jnp.zeros((rows, LANES), jnp.float32)
        full[z, 8 : 8 + rows, LANES + cols :] = jnp.zeros((rows, LANES), jnp.float32)

        @pl.loop(0, rows // 16)
        def _(i):
            r = pl.multiple_of(i * 16, 16)
            full[z, pl.ds(pl.multiple_of(r + 8, 8), 16), LANES : LANES + cols] = dens[
                z, pl.ds(r, 16), :
            ].astype(jnp.float32)

    pl.semaphore_wait(
        barrier, bricks - 1 + jnp.where(has_low, 1, 0) + jnp.where(has_high, 1, 0)
    )

    def halo_copy(side):
        return pltpu.make_async_remote_copy(
            src_ref=halo_out.at[side],
            dst_ref=halo_in.at[1 - side],
            send_sem=halo_send.at[side],
            recv_sem=halo_recv.at[1 - side],
            device_id=(me, scr + 2 * side - 1),
            device_id_type=MESH,
        )

    def halo_wait(side):
        pltpu.make_async_remote_copy(
            src_ref=halo_out.at[side],
            dst_ref=halo_in.at[side],
            send_sem=halo_send.at[side],
            recv_sem=halo_recv.at[side],
            device_id=(me, scr + 2 * side - 1),
            device_id_type=MESH,
        ).wait_recv()

    @pl.when(has_low)
    def _():
        halo_copy(0).start()

    @pl.when(has_high)
    def _():
        halo_copy(1).start()

    def pixel_tile(r, c):
        def tile(z, dr, dc):
            return full[
                z,
                pl.ds(pl.multiple_of(r + 8 + dr * 8, 8), 8),
                pl.ds(pl.multiple_of(c + (1 + dc) * LANES, LANES), LANES),
            ]

        through = jnp.ones((8, LANES), jnp.float32)
        tau = jnp.zeros((8, LANES), jnp.float32)
        sums = [jnp.zeros((8, LANES), jnp.float32) for _ in range(3)]
        before, here = tile(0, 0, 0), tile(1, 0, 0)
        for z in range(slices):
            after = tile(z + 2, 0, 0)
            left = pltpu.roll(jnp.where(lane == LANES - 1, tile(z + 1, 0, -1), here), 1, 1)
            right = pltpu.roll(jnp.where(lane == 0, tile(z + 1, 0, 1), here), LANES - 1, 1)
            up = pltpu.roll(jnp.where(sub == 7, tile(z + 1, -1, 0), here), 1, 0)
            down = pltpu.roll(jnp.where(sub == 0, tile(z + 1, 1, 0), here), 7, 0)
            dx, dy, dz = right - left, down - up, after - before
            square = (dx * dx + dy * dy) + (dz * dz + 4.0)
            lit = (0.45 * LIGHT[0]) * dx + (0.45 * LIGHT[1]) * dy + (0.45 * LIGHT[2]) * dz
            shade = 0.55 + lit * lax.rsqrt(square)
            kinds = mat[z, pl.ds(r, 8), pl.ds(c, LANES)]

            def pick(values):
                return jnp.take_along_axis(values, kinds, axis=1, mode="promise_in_bounds")

            whole = 1.0 + here
            guess = pl.reciprocal(whole, approx=True)
            sigma = pick(ext2) * (here * (guess * (2.0 - whole * guess)))
            later = through * jnp.exp2(-sigma)
            weight = (through - later) * shade
            for k in range(3):
                sums[k] = sums[k] + weight * pick(tabs[k])
            tau = tau + sigma
            through = later
            before, here = here, after
        gain = 1.0 / (1.0 - through)
        values = [s * gain for s in sums] + [tau]
        codes = [
            jnp.minimum(v * s + 0.5, 65535.0).astype(jnp.int32) for v, s in zip(values, scales)
        ]
        return [(codes[0] << 16) | codes[1], (codes[2] << 16) | codes[3]]

    def row_group(unit_at, g):
        r = pl.multiple_of(unit_at * unit + g * 8, 8)

        @pl.loop(0, cols // (LANES * CHUNKS))
        def _(i):
            for k in range(CHUNKS):
                c = pl.multiple_of(i * (LANES * CHUNKS) + k * LANES, LANES)
                words = pixel_tile(r, c)
                for p in range(2):
                    for h in range(8 // part):
                        sendbuf[
                            unit_at * (unit // part) + g * (8 // part) + h, p, :, pl.ds(c, LANES)
                        ] = words[p][h * part : (h + 1) * part]

    def strip_copy(s, first=None, count=blocks):
        first = s * blocks if first is None else first
        return pltpu.make_async_remote_copy(
            src_ref=sendbuf.at[pl.ds(first, count)],
            dst_ref=recv.at[me, pl.ds(first - s * blocks, count)],
            send_sem=send_sem.at[s],
            recv_sem=recv_sem.at[me],
            device_id=(s, scr),
            device_id_type=MESH,
        )

    def own_copy(first, count):
        return pltpu.make_async_copy(
            sendbuf.at[pl.ds(first, count)],
            recv.at[me, pl.ds(first - me * blocks, count)],
            own_sem,
        )

    def pieces(group):
        runs = {}
        for b in range(group * (8 // part), (group + 1) * (8 // part)):
            runs.setdefault(b // blocks, []).append(b)
        return [(k, held[0], len(held)) for k, held in runs.items()]

    def send(s, first, count, j):
        if j < units - 1:
            strip_copy(s, first, count).start()
        else:
            @pl.when(s != me)
            def _():
                strip_copy(s, first, count).start()

            @pl.when(s == me)
            def _():
                own_copy(first, count).start()

    def set_halo(side, there):
        row = 7 if side == 0 else 8 + rows

        @pl.when(there)
        def _():
            halo_wait(side)
            for z in range(slices):
                full[z + 1, row : row + 1, LANES : LANES + cols] = halo_in[side, z : z + 1, :]

        @pl.when(jnp.logical_not(there))
        def _():
            for z in range(slices):
                full[z + 1, row : row + 1, LANES : LANES + cols] = jnp.zeros(
                    (1, cols), jnp.float32
                )

    for j in range(units):
        at = visits[j]
        mat_copy(j).wait()

        @pl.loop(0, groups)
        def _(i):
            @pl.when(jnp.logical_and(i == groups - 1, at == 0))
            def _():
                set_halo(0, has_low)

            @pl.when(jnp.logical_and(i == groups - 1, at == units - 1))
            def _():
                set_halo(1, has_high)

            g = jnp.where(at == 0, groups - 1 - i, i)
            row_group(at, g)
            for group in range(groups):
                @pl.when(g == group)
                def _():
                    for k, first, count in pieces(group):
                        send(at * per_unit + k, at * (unit // part) + first, count, j)

    def brick_at(rank):
        def step(j, found):
            return jnp.maximum(found, jnp.where(order_ref[j] == rank, j, 0))

        return lax.fori_loop(0, bricks, step, jnp.int32(0), unroll=bricks <= 8)

    at_rank = [brick_at(i) for i in range(bricks)]

    own_copy(me * blocks, blocks).wait()
    for peer in range(bricks):
        @pl.when(me != peer)
        def _():
            pltpu.make_async_remote_copy(
                src_ref=sendbuf.at[pl.ds(peer * blocks, blocks)],
                dst_ref=recv.at[peer],
                send_sem=send_sem.at[peer],
                recv_sem=recv_sem.at[peer],
                device_id=(peer, scr),
                device_id_type=MESH,
            ).wait_recv()

    width = 4 * LANES
    unscale = [jnp.concatenate([s[:part]] * (width // LANES), axis=1) for s in steps]
    for b in range(blocks):
        @pl.loop(0, cols // width)
        def _(i):
            where = pl.ds(pl.multiple_of(i * width, width), width)
            through = jnp.ones((part, width), jnp.float32)
            sums = [jnp.zeros((part, width), jnp.float32) for _ in range(3)]
            for rank in range(bricks):
                first = recv[at_rank[rank], b, 0, :, where]
                second = recv[at_rank[rank], b, 1, :, where]
                codes = []
                for word in (first, second):
                    codes += [lax.shift_right_logical(word, 16), word & 0xFFFF]
                values = [k.astype(jnp.float32) * s for k, s in zip(codes, unscale)]
                later = through * jnp.exp2(-values[3])
                weight = through - later
                sums = [a + weight * v for a, v in zip(sums, values[:3])]
                through = later
            for k, value in enumerate(sums + [1.0 - through]):
                for row in range(part):
                    out_ref[b * part + row, k : k + 1, where] = value[row : row + 1]

    for peer in range(bricks):
        @pl.when(me != peer)
        def _():
            strip_copy(peer).wait_send()

    @pl.when(has_low)
    def _():
        halo_copy(0).wait_send()

    @pl.when(has_high)
    def _():
        halo_copy(1).wait_send()


def solution(mesh):
    bricks, screens = mesh.shape["depth"], mesh.shape["screen"]

    def body(density, material, order, color_table, extinction):
        stored, rows, cols = density.shape
        slices = stored - 2
        strip = rows // bricks
        part = math.gcd(8, strip)
        blocks = strip // part
        hbm = pl.BlockSpec(memory_space=pl.ANY)
        voxels = slices * rows * cols
        image = pl.pallas_call(
            functools.partial(kernel, bricks, screens, strip),
            out_shape=jax.ShapeDtypeStruct((strip, 4, cols), jnp.float32),
            in_specs=[hbm] * 5,
            out_specs=pl.BlockSpec(memory_space=pltpu.VMEM),
            scratch_shapes=[
                pltpu.VMEM((stored, rows, cols), jnp.bfloat16),
                pltpu.VMEM((stored, rows + 16, cols + 2 * LANES), jnp.float32),
                pltpu.VMEM((slices, rows, cols), jnp.int32),
                pltpu.VMEM((rows // part, 2, part, cols), jnp.int32),
                pltpu.VMEM((bricks, blocks, 2, part, cols), jnp.int32),
                pltpu.VMEM((2, slices, cols), jnp.float32),
                pltpu.VMEM((2, slices, cols), jnp.float32),
                pltpu.SemaphoreType.DMA((2,)),
                pltpu.SemaphoreType.DMA((rows // math.lcm(8, strip),)),
                pltpu.SemaphoreType.DMA((2,)),
                pltpu.SemaphoreType.DMA((2,)),
                pltpu.SemaphoreType.DMA((bricks,)),
                pltpu.SemaphoreType.DMA((bricks,)),
                pltpu.SemaphoreType.DMA,
                pltpu.SMEM((bricks,), jnp.int32),
                pltpu.SMEM(color_table.shape[::-1], jnp.float32),
                pltpu.SMEM(extinction.shape, jnp.float32),
                pltpu.SemaphoreType.DMA((3,)),
            ],
            compiler_params=pltpu.CompilerParams(
                collective_id=0, has_side_effects=True, vmem_limit_bytes=64 * 1024 * 1024
            ),
            cost_estimate=pl.CostEstimate(
                flops=60 * voxels, bytes_accessed=7 * voxels, transcendentals=3 * voxels
            ),
        )(density, material, order, color_table.T, extinction)
        return image.transpose(1, 0, 2)

    placed = (P("depth", "screen", None), P("depth", "screen", None), P(), P(), P())
    return jax.shard_map(
        body,
        mesh=mesh,
        in_specs=placed,
        out_specs=P(None, ("screen", "depth"), None),
        check_vma=False,
    )
```

```python
import functools
import math
import jax
import jax.numpy as jnp
from jax import lax
from jax.experimental import pallas as pl
from jax.experimental.pallas import tpu as pltpu
from jax.sharding import PartitionSpec as P

LIGHT = (0.48, 0.6, 0.64)
MESH = pl.DeviceIdType.MESH
LANES = 128
CODE_TOP = 65000.0
CHUNKS = 4


def kernel(
    bricks, screens, strip,
    dens_hbm, mat_hbm, order_hbm, color_hbm, ext_hbm, out_ref,
    dens, full, mat, sendbuf, recv, halo_out, halo_in,
    dens_sem, mat_sem, halo_send, halo_recv, send_sem, recv_sem, own_sem,
    order_ref, color_ref, ext_ref, small_sem,
):
    stored, rows, cols = dens.shape
    slices = stored - 2
    unit = math.lcm(8, strip)
    units = rows // unit
    groups = unit // 8
    per_unit = unit // strip
    wide = sendbuf.shape[3]
    fold = cols // wide
    part = 8 // fold
    runs = max(1, CHUNKS // fold)
    blocks = strip // part
    entries = ext_ref.shape[0]

    me = lax.axis_index("depth")
    scr = lax.axis_index("screen")
    has_low = scr > 0
    has_high = scr < screens - 1

    own = (me * strip) // unit
    if units == 4:
        visits = [3 - own, own + 1 - 2 * (own % 2), (own + 2) % 4, own]
    else:
        visits = [(own + 1 + j) % units for j in range(units)]

    def dens_copy(z):
        return pltpu.make_async_copy(dens_hbm.at[z], dens.at[z], dens_sem.at[z])

    def mat_copy(j):
        where = pl.ds(pl.multiple_of(visits[j] * unit, 8), unit)
        return pltpu.make_async_copy(mat_hbm.at[:, where], mat.at[:, where], mat_sem.at[j])

    small = [
        pltpu.make_async_copy(src, dst, small_sem.at[i])
        for i, (src, dst) in enumerate(
            [(order_hbm, order_ref), (color_hbm, color_ref), (ext_hbm, ext_ref)]
        )
    ]
    for copy in small:
        copy.start()
    for z in range(stored):
        dens_copy(z).start()
    mat_copy(0).start()

    barrier = pltpu.get_barrier_semaphore()
    for peer in range(bricks):
        @pl.when(me != peer)
        def _():
            pl.semaphore_signal(barrier, inc=1, device_id=(peer, scr), device_id_type=MESH)

    @pl.when(has_low)
    def _():
        pl.semaphore_signal(barrier, inc=1, device_id=(me, scr - 1), device_id_type=MESH)

    @pl.when(has_high)
    def _():
        pl.semaphore_signal(barrier, inc=1, device_id=(me, scr + 1), device_id_type=MESH)

    for copy in small:
        copy.wait()

    lane = lax.broadcasted_iota(jnp.int32, (8, LANES), 1)
    sub = lax.broadcasted_iota(jnp.int32, (8, LANES), 0)

    def table(read):
        out = jnp.zeros((8, LANES), jnp.float32)
        for e in range(entries):
            out = jnp.where(lane == e, read(e), out)
        return out

    tabs = [table(lambda e, c=c: color_ref[c, e]) for c in range(3)]
    ext2 = table(lambda e: ext_ref[e]) * math.log2(math.e)
    tops = [jnp.max(t, axis=1, keepdims=True) for t in tabs]
    top_tau = slices * jnp.max(ext2, axis=1, keepdims=True)
    steps = [jnp.broadcast_to(t * (1.0 / CODE_TOP), (8, LANES)) for t in tops + [top_tau]]
    scales = [1.0 / s for s in steps]

    for z in range(stored):
        dens_copy(z).wait()
        if z == stored - 1:
            for j in range(1, units):
                mat_copy(j).start()
        full[z, 8 : 8 + rows, 0:LANES] = jnp.zeros((rows, LANES), jnp.float32)
        full[z, 8 : 8 + rows, LANES + cols :] = jnp.zeros((rows, LANES), jnp.float32)

        @pl.loop(0, rows // 32)
        def _(i):
            r = pl.multiple_of(i * 32, 32)
            full[z, pl.ds(pl.multiple_of(r + 8, 8), 32), LANES : LANES + cols] = dens[
                z, pl.ds(r, 32), :
            ].astype(jnp.float32)

        if 0 < z <= slices:
            halo_out[0, z - 1 : z, :] = full[z, 8:9, LANES : LANES + cols]
            halo_out[1, z - 1 : z, :] = full[z, 7 + rows : 8 + rows, LANES : LANES + cols]

    pl.semaphore_wait(
        barrier, bricks - 1 + jnp.where(has_low, 1, 0) + jnp.where(has_high, 1, 0)
    )

    def halo_copy(side):
        return pltpu.make_async_remote_copy(
            src_ref=halo_out.at[side],
            dst_ref=halo_in.at[1 - side],
            send_sem=halo_send.at[side],
            recv_sem=halo_recv.at[1 - side],
            device_id=(me, scr + 2 * side - 1),
            device_id_type=MESH,
        )

    def halo_wait(side):
        pltpu.make_async_remote_copy(
            src_ref=halo_out.at[side],
            dst_ref=halo_in.at[side],
            send_sem=halo_send.at[side],
            recv_sem=halo_recv.at[side],
            device_id=(me, scr + 2 * side - 1),
            device_id_type=MESH,
        ).wait_recv()

    @pl.when(has_low)
    def _():
        halo_copy(0).start()

    @pl.when(has_high)
    def _():
        halo_copy(1).start()

    def pixel_tile(r, c):
        def tile(z, dr, dc):
            return full[
                z,
                pl.ds(pl.multiple_of(r + 8 + dr * 8, 8), 8),
                pl.ds(pl.multiple_of(c + (1 + dc) * LANES, LANES), LANES),
            ]

        through = jnp.ones((8, LANES), jnp.float32)
        tau = jnp.zeros((8, LANES), jnp.float32)
        sums = [jnp.zeros((8, LANES), jnp.float32) for _ in range(3)]
        before, here = tile(0, 0, 0), tile(1, 0, 0)
        for z in range(slices):
            after = tile(z + 2, 0, 0)
            left = pltpu.roll(jnp.where(lane == LANES - 1, tile(z + 1, 0, -1), here), 1, 1)
            right = pltpu.roll(jnp.where(lane == 0, tile(z + 1, 0, 1), here), LANES - 1, 1)
            up = pltpu.roll(jnp.where(sub == 7, tile(z + 1, -1, 0), here), 1, 0)
            down = pltpu.roll(jnp.where(sub == 0, tile(z + 1, 1, 0), here), 7, 0)
            dx, dy, dz = right - left, down - up, after - before
            square = (dx * dx + dy * dy) + (dz * dz + 4.0)
            lit = (0.45 * LIGHT[0]) * dx + (0.45 * LIGHT[1]) * dy + (0.45 * LIGHT[2]) * dz
            shade = 0.55 + lit * lax.rsqrt(square)
            kinds = mat[z, pl.ds(r, 8), pl.ds(c, LANES)]

            def pick(values):
                return jnp.take_along_axis(values, kinds, axis=1, mode="promise_in_bounds")

            whole = 1.0 + here
            guess = pl.reciprocal(whole, approx=True)
            sigma = pick(ext2) * (here * (guess * (2.0 - whole * guess)))
            later = through * jnp.exp2(-sigma)
            weight = (through - later) * shade
            for k in range(3):
                sums[k] = sums[k] + weight * pick(tabs[k])
            tau = tau + sigma
            through = later
            before, here = here, after
        gain = 1.0 / (1.0 - through)
        values = [s * gain for s in sums] + [tau]
        codes = [
            jnp.minimum(v * s + 0.5, 65535.0).astype(jnp.int32) for v, s in zip(values, scales)
        ]
        return [(codes[0] << 16) | codes[1], (codes[2] << 16) | codes[3]]

    def row_group(unit_at, g):
        r = pl.multiple_of(unit_at * unit + g * 8, 8)

        @pl.loop(0, wide // (LANES * runs))
        def _(i):
            for k in range(runs):
                c = pl.multiple_of(i * (LANES * runs) + k * LANES, LANES)
                tiles = [pixel_tile(r, pl.multiple_of(f * wide + c, LANES)) for f in range(fold)]
                for h in range(fold):
                    at = unit_at * (unit // part) + g * fold + h
                    for p in range(2):
                        sendbuf[at, p, :, pl.ds(c, LANES)] = jnp.concatenate(
                            [words[p][h * part : (h + 1) * part] for words in tiles], axis=0
                        )

    def strip_copy(s, first=None, count=blocks):
        first = s * blocks if first is None else first
        return pltpu.make_async_remote_copy(
            src_ref=sendbuf.at[pl.ds(first, count)],
            dst_ref=recv.at[me, pl.ds(first - s * blocks, count)],
            send_sem=send_sem.at[s],
            recv_sem=recv_sem.at[me],
            device_id=(s, scr),
            device_id_type=MESH,
        )

    def own_copy(first, count):
        return pltpu.make_async_copy(
            sendbuf.at[pl.ds(first, count)],
            recv.at[me, pl.ds(first - me * blocks, count)],
            own_sem,
        )

    def pieces(group):
        runs = {}
        for b in range(group * (8 // part), (group + 1) * (8 // part)):
            runs.setdefault(b // blocks, []).append(b)
        return [(k, held[0], len(held)) for k, held in runs.items()]

    def send(s, first, count, j):
        if j < units - 1:
            strip_copy(s, first, count).start()
        else:
            @pl.when(s != me)
            def _():
                strip_copy(s, first, count).start()

            @pl.when(s == me)
            def _():
                own_copy(first, count).start()

    def set_halo(side, there):
        row = 7 if side == 0 else 8 + rows

        @pl.when(there)
        def _():
            halo_wait(side)
            for z in range(slices):
                full[z + 1, row : row + 1, LANES : LANES + cols] = halo_in[side, z : z + 1, :]

        @pl.when(jnp.logical_not(there))
        def _():
            for z in range(slices):
                full[z + 1, row : row + 1, LANES : LANES + cols] = jnp.zeros(
                    (1, cols), jnp.float32
                )

    for j in range(units):
        at = visits[j]
        mat_copy(j).wait()

        @pl.loop(0, groups)
        def _(i):
            @pl.when(jnp.logical_and(i == groups - 1, at == 0))
            def _():
                set_halo(0, has_low)

            @pl.when(jnp.logical_and(i == groups - 1, at == units - 1))
            def _():
                set_halo(1, has_high)

            g = jnp.where(at == 0, groups - 1 - i, i)
            row_group(at, g)
            for group in range(groups):
                @pl.when(g == group)
                def _():
                    for k, first, count in pieces(group):
                        send(at * per_unit + k, at * (unit // part) + first, count, j)

    def brick_at(rank):
        def step(j, found):
            return jnp.maximum(found, jnp.where(order_ref[j] == rank, j, 0))

        return lax.fori_loop(0, bricks, step, jnp.int32(0), unroll=bricks <= 8)

    at_rank = [brick_at(i) for i in range(bricks)]

    own_copy(me * blocks, blocks).wait()
    for peer in range(bricks):
        @pl.when(me != peer)
        def _():
            pltpu.make_async_remote_copy(
                src_ref=sendbuf.at[pl.ds(peer * blocks, blocks)],
                dst_ref=recv.at[peer],
                send_sem=send_sem.at[peer],
                recv_sem=recv_sem.at[peer],
                device_id=(peer, scr),
                device_id_type=MESH,
            ).wait_recv()

    width = 2 * LANES
    unscale = [jnp.concatenate([s] * (width // LANES), axis=1) for s in steps]
    for b in range(blocks):
        @pl.loop(0, wide // width)
        def _(i):
            where = pl.ds(pl.multiple_of(i * width, width), width)
            through = jnp.ones((8, width), jnp.float32)
            sums = [jnp.zeros((8, width), jnp.float32) for _ in range(3)]
            for rank in range(bricks):
                first = recv[at_rank[rank], b, 0, :, where]
                second = recv[at_rank[rank], b, 1, :, where]
                codes = []
                for word in (first, second):
                    codes += [lax.shift_right_logical(word, 16), word & 0xFFFF]
                values = [k.astype(jnp.float32) * s for k, s in zip(codes, unscale)]
                later = through * jnp.exp2(-values[3])
                weight = through - later
                sums = [a + weight * v for a, v in zip(sums, values[:3])]
                through = later
            for k, value in enumerate(sums + [1.0 - through]):
                for f in range(fold):
                    to = pl.ds(pl.multiple_of(f * wide + i * width, width), width)
                    for row in range(part):
                        spot = f * part + row
                        out_ref[b * part + row, k : k + 1, to] = value[spot : spot + 1]

    for peer in range(bricks):
        @pl.when(me != peer)
        def _():
            strip_copy(peer).wait_send()

    @pl.when(has_low)
    def _():
        halo_copy(0).wait_send()

    @pl.when(has_high)
    def _():
        halo_copy(1).wait_send()


def solution(mesh):
    bricks, screens = mesh.shape["depth"], mesh.shape["screen"]

    def body(density, material, order, color_table, extinction):
        stored, rows, cols = density.shape
        slices = stored - 2
        strip = rows // bricks
        part = math.gcd(8, strip)
        blocks = strip // part
        hbm = pl.BlockSpec(memory_space=pl.ANY)
        voxels = slices * rows * cols
        image = pl.pallas_call(
            functools.partial(kernel, bricks, screens, strip),
            out_shape=jax.ShapeDtypeStruct((strip, 4, cols), jnp.float32),
            in_specs=[hbm] * 5,
            out_specs=pl.BlockSpec(memory_space=pltpu.VMEM),
            scratch_shapes=[
                pltpu.VMEM((stored, rows, cols), jnp.bfloat16),
                pltpu.VMEM((stored, rows + 16, cols + 2 * LANES), jnp.float32),
                pltpu.VMEM((slices, rows, cols), jnp.int32),
                pltpu.VMEM((rows // part, 2, 8, cols * part // 8), jnp.int32),
                pltpu.VMEM((bricks, blocks, 2, 8, cols * part // 8), jnp.int32),
                pltpu.VMEM((2, slices, cols), jnp.float32),
                pltpu.VMEM((2, slices, cols), jnp.float32),
                pltpu.SemaphoreType.DMA((stored,)),
                pltpu.SemaphoreType.DMA((rows // math.lcm(8, strip),)),
                pltpu.SemaphoreType.DMA((2,)),
                pltpu.SemaphoreType.DMA((2,)),
                pltpu.SemaphoreType.DMA((bricks,)),
                pltpu.SemaphoreType.DMA((bricks,)),
                pltpu.SemaphoreType.DMA,
                pltpu.SMEM((bricks,), jnp.int32),
                pltpu.SMEM(color_table.shape[::-1], jnp.float32),
                pltpu.SMEM(extinction.shape, jnp.float32),
                pltpu.SemaphoreType.DMA((3,)),
            ],
            compiler_params=pltpu.CompilerParams(
                collective_id=0, has_side_effects=True, vmem_limit_bytes=64 * 1024 * 1024
            ),
            cost_estimate=pl.CostEstimate(
                flops=60 * voxels, bytes_accessed=7 * voxels, transcendentals=3 * voxels
            ),
        )(density, material, order, color_table.T, extinction)
        return image.transpose(1, 0, 2)

    placed = (P("depth", "screen", None), P("depth", "screen", None), P(), P(), P())
    return jax.shard_map(
        body,
        mesh=mesh,
        in_specs=placed,
        out_specs=P(None, ("screen", "depth"), None),
        check_vma=False,
    )
```

```python
import functools
import math
import jax
import jax.numpy as jnp
from jax import lax
from jax.experimental import pallas as pl
from jax.experimental.pallas import tpu as pltpu
from jax.sharding import PartitionSpec as P

LIGHT = (0.48, 0.6, 0.64)
MESH = pl.DeviceIdType.MESH
LANES = 128
CODE_TOP = 65000.0
CHUNKS = 4


def kernel(
    bricks, screens, strip,
    dens_hbm, mat_hbm, order_hbm, color_hbm, ext_hbm, out_ref,
    dens, full, mat, sendbuf, recv, halo_out, halo_in,
    dens_sem, mat_sem, halo_send, halo_recv, send_sem, recv_sem, own_sem,
    order_ref, color_ref, ext_ref, small_sem,
):
    stored, rows, cols = dens.shape
    slices = stored - 2
    unit = math.lcm(8, strip)
    units = rows // unit
    groups = unit // 8
    per_unit = unit // strip
    wide = sendbuf.shape[3]
    fold = cols // wide
    part = 8 // fold
    runs = max(1, CHUNKS // fold)
    blocks = strip // part
    entries = ext_ref.shape[0]

    me = lax.axis_index("depth")
    scr = lax.axis_index("screen")
    has_low = scr > 0
    has_high = scr < screens - 1

    own = (me * strip) // unit
    if units == 4:
        visits = [3 - own, own + 1 - 2 * (own % 2), (own + 2) % 4, own]
    else:
        visits = [(own + 1 + j) % units for j in range(units)]

    def dens_copy(z):
        return pltpu.make_async_copy(dens_hbm.at[z], dens.at[z], dens_sem.at[z])

    def mat_copy(j):
        where = pl.ds(pl.multiple_of(visits[j] * unit, 8), unit)
        return pltpu.make_async_copy(mat_hbm.at[:, where], mat.at[:, where], mat_sem.at[j])

    small = [
        pltpu.make_async_copy(src, dst, small_sem.at[i])
        for i, (src, dst) in enumerate(
            [(order_hbm, order_ref), (color_hbm, color_ref), (ext_hbm, ext_ref)]
        )
    ]
    for copy in small:
        copy.start()
    for z in range(stored):
        dens_copy(z).start()
    mat_copy(0).start()

    barrier = pltpu.get_barrier_semaphore()
    for peer in range(bricks):
        @pl.when(me != peer)
        def _():
            pl.semaphore_signal(barrier, inc=1, device_id=(peer, scr), device_id_type=MESH)

    @pl.when(has_low)
    def _():
        pl.semaphore_signal(barrier, inc=1, device_id=(me, scr - 1), device_id_type=MESH)

    @pl.when(has_high)
    def _():
        pl.semaphore_signal(barrier, inc=1, device_id=(me, scr + 1), device_id_type=MESH)

    for copy in small:
        copy.wait()

    lane = lax.broadcasted_iota(jnp.int32, (8, LANES), 1)

    def table(read):
        out = jnp.zeros((8, LANES), jnp.float32)
        for e in range(entries):
            out = jnp.where(lane == e, read(e), out)
        return out

    tabs = [table(lambda e, c=c: color_ref[c, e]) for c in range(3)]
    ext2 = table(lambda e: ext_ref[e]) * math.log2(math.e)
    tops = [jnp.max(t, axis=1, keepdims=True) for t in tabs]
    top_tau = slices * jnp.max(ext2, axis=1, keepdims=True)
    steps = [jnp.broadcast_to(t * (1.0 / CODE_TOP), (8, LANES)) for t in tops + [top_tau]]
    scales = [1.0 / s for s in steps]

    for z in range(stored):
        dens_copy(z).wait()
        if z == stored - 1:
            for j in range(1, units):
                mat_copy(j).start()
        for edge in (0, cols // LANES + 1):
            full[z, edge, 8 : 8 + rows, :] = jnp.zeros((rows, LANES), jnp.float32)

        @pl.loop(0, rows // 32)
        def _(i):
            r = pl.multiple_of(i * 32, 32)
            for k in range(cols // LANES):
                full[z, 1 + k, pl.ds(pl.multiple_of(r + 8, 8), 32), :] = dens[
                    z, pl.ds(r, 32), k * LANES : (k + 1) * LANES
                ].astype(jnp.float32)

        if 0 < z <= slices:
            halo_out[0, z - 1 : z, :] = dens[z, 0:16, :].astype(jnp.float32)[0:1]
            halo_out[1, z - 1 : z, :] = dens[z, rows - 16 : rows, :].astype(jnp.float32)[15:16]

    pl.semaphore_wait(
        barrier, bricks - 1 + jnp.where(has_low, 1, 0) + jnp.where(has_high, 1, 0)
    )

    def halo_copy(side):
        return pltpu.make_async_remote_copy(
            src_ref=halo_out.at[side],
            dst_ref=halo_in.at[1 - side],
            send_sem=halo_send.at[side],
            recv_sem=halo_recv.at[1 - side],
            device_id=(me, scr + 2 * side - 1),
            device_id_type=MESH,
        )

    def halo_wait(side):
        pltpu.make_async_remote_copy(
            src_ref=halo_out.at[side],
            dst_ref=halo_in.at[side],
            send_sem=halo_send.at[side],
            recv_sem=halo_recv.at[side],
            device_id=(me, scr + 2 * side - 1),
            device_id_type=MESH,
        ).wait_recv()

    @pl.when(has_low)
    def _():
        halo_copy(0).start()

    @pl.when(has_high)
    def _():
        halo_copy(1).start()

    def pixel_tile(r, chunk):
        c = pl.multiple_of(chunk * LANES, LANES)

        def tile(z, dr, dc):
            first = r + 8 + dr
            return full[
                z, chunk + 1 + dc, pl.ds(first if dr else pl.multiple_of(first, 8), 8), :
            ]

        through = jnp.ones((8, LANES), jnp.float32)
        tau = jnp.zeros((8, LANES), jnp.float32)
        sums = [jnp.zeros((8, LANES), jnp.float32) for _ in range(3)]
        before, here = tile(0, 0, 0), tile(1, 0, 0)
        for z in range(slices):
            after = tile(z + 2, 0, 0)
            left = pltpu.roll(jnp.where(lane == LANES - 1, tile(z + 1, 0, -1), here), 1, 1)
            right = pltpu.roll(jnp.where(lane == 0, tile(z + 1, 0, 1), here), LANES - 1, 1)
            up = tile(z + 1, -1, 0)
            down = tile(z + 1, 1, 0)
            dx, dy, dz = right - left, down - up, after - before
            square = (dx * dx + dy * dy) + (dz * dz + 4.0)
            lit = (0.45 * LIGHT[0]) * dx + (0.45 * LIGHT[1]) * dy + (0.45 * LIGHT[2]) * dz
            shade = 0.55 + lit * lax.rsqrt(square)
            kinds = mat[z, pl.ds(r, 8), pl.ds(c, LANES)]

            def pick(values):
                return jnp.take_along_axis(values, kinds, axis=1, mode="promise_in_bounds")

            whole = 1.0 + here
            guess = pl.reciprocal(whole, approx=True)
            sigma = pick(ext2) * (here * (guess * (2.0 - whole * guess)))
            later = through * jnp.exp2(-sigma)
            weight = (through - later) * shade
            for k in range(3):
                sums[k] = sums[k] + weight * pick(tabs[k])
            tau = tau + sigma
            through = later
            before, here = here, after
        gain = 1.0 / (1.0 - through)
        values = [s * gain for s in sums] + [tau]
        codes = [
            jnp.minimum(v * s + 0.5, 65535.0).astype(jnp.int32) for v, s in zip(values, scales)
        ]
        return [(codes[0] << 16) | codes[1], (codes[2] << 16) | codes[3]]

    def row_group(unit_at, g):
        r = pl.multiple_of(unit_at * unit + g * 8, 8)

        @pl.loop(0, wide // (LANES * runs))
        def _(i):
            for k in range(runs):
                c = pl.multiple_of(i * (LANES * runs) + k * LANES, LANES)
                tiles = [pixel_tile(r, f * (wide // LANES) + i * runs + k) for f in range(fold)]
                for h in range(fold):
                    at = unit_at * (unit // part) + g * fold + h
                    for p in range(2):
                        sendbuf[at, p, :, pl.ds(c, LANES)] = jnp.concatenate(
                            [words[p][h * part : (h + 1) * part] for words in tiles], axis=0
                        )

    def block_copy(s, b):
        return pltpu.make_async_remote_copy(
            src_ref=sendbuf.at[s * blocks + b],
            dst_ref=recv[b].at[me],
            send_sem=send_sem.at[s, b],
            recv_sem=recv_sem.at[me, b],
            device_id=(s, scr),
            device_id_type=MESH,
        )

    def own_copy(b):
        return pltpu.make_async_copy(
            sendbuf.at[me * blocks + b], recv[b].at[me], own_sem.at[b]
        )

    def send(s, b, j):
        if j < units - 1:
            block_copy(s, b).start()
        else:
            @pl.when(s != me)
            def _():
                block_copy(s, b).start()

            @pl.when(s == me)
            def _():
                own_copy(b).start()

    def set_halo(side, there):
        row = 7 if side == 0 else 8 + rows

        @pl.when(there)
        def _():
            halo_wait(side)
            for z in range(slices):
                for k in range(cols // LANES):
                    full[z + 1, 1 + k, row : row + 1, :] = halo_in[
                        side, z : z + 1, k * LANES : (k + 1) * LANES
                    ]

        @pl.when(jnp.logical_not(there))
        def _():
            for z in range(slices):
                for k in range(cols // LANES):
                    full[z + 1, 1 + k, row : row + 1, :] = jnp.zeros((1, LANES), jnp.float32)

    for j in range(units):
        at = visits[j]
        mat_copy(j).wait()

        @pl.loop(0, groups)
        def _(i):
            @pl.when(jnp.logical_and(i == groups - 1, at == 0))
            def _():
                set_halo(0, has_low)

            @pl.when(jnp.logical_and(i == groups - 1, at == units - 1))
            def _():
                set_halo(1, has_high)

            g = jnp.where(at == 0, groups - 1 - i, i)
            row_group(at, g)
            for group in range(groups):
                @pl.when(g == group)
                def _():
                    for b in range(group * fold, (group + 1) * fold):
                        send(at * per_unit + b // blocks, b % blocks, j)

    def brick_at(rank):
        def step(j, found):
            return jnp.maximum(found, jnp.where(order_ref[j] == rank, j, 0))

        return lax.fori_loop(0, bricks, step, jnp.int32(0), unroll=bricks <= 8)

    at_rank = [brick_at(i) for i in range(bricks)]

    width = 2 * LANES
    unscale = [jnp.concatenate([s] * (width // LANES), axis=1) for s in steps]
    for b in range(blocks):
        own_copy(b).wait()
        for peer in range(bricks):
            @pl.when(me != peer)
            def _():
                pltpu.make_async_remote_copy(
                    src_ref=sendbuf.at[peer * blocks + b],
                    dst_ref=recv[b].at[peer],
                    send_sem=send_sem.at[peer, b],
                    recv_sem=recv_sem.at[peer, b],
                    device_id=(peer, scr),
                    device_id_type=MESH,
                ).wait_recv()

        @pl.loop(0, wide // width)
        def _(i):
            where = pl.ds(pl.multiple_of(i * width, width), width)
            through = jnp.ones((8, width), jnp.float32)
            sums = [jnp.zeros((8, width), jnp.float32) for _ in range(3)]
            for rank in range(bricks):
                first = recv[b][at_rank[rank], 0, :, where]
                second = recv[b][at_rank[rank], 1, :, where]
                codes = []
                for word in (first, second):
                    codes += [lax.shift_right_logical(word, 16), word & 0xFFFF]
                values = [k.astype(jnp.float32) * s for k, s in zip(codes, unscale)]
                later = through * jnp.exp2(-values[3])
                weight = through - later
                sums = [a + weight * v for a, v in zip(sums, values[:3])]
                through = later
            for k, value in enumerate(sums + [1.0 - through]):
                for f in range(fold):
                    to = pl.ds(pl.multiple_of(f * wide + i * width, width), width)
                    for row in range(part):
                        spot = f * part + row
                        out_ref[b * part + row, k : k + 1, to] = value[spot : spot + 1]

    for peer in range(bricks):
        @pl.when(me != peer)
        def _():
            for b in range(blocks):
                block_copy(peer, b).wait_send()

    @pl.when(has_low)
    def _():
        halo_copy(0).wait_send()

    @pl.when(has_high)
    def _():
        halo_copy(1).wait_send()


def solution(mesh):
    bricks, screens = mesh.shape["depth"], mesh.shape["screen"]

    def body(density, material, order, color_table, extinction):
        stored, rows, cols = density.shape
        slices = stored - 2
        strip = rows // bricks
        part = math.gcd(8, strip)
        blocks = strip // part
        hbm = pl.BlockSpec(memory_space=pl.ANY)
        voxels = slices * rows * cols
        image = pl.pallas_call(
            functools.partial(kernel, bricks, screens, strip),
            out_shape=jax.ShapeDtypeStruct((strip, 4, cols), jnp.float32),
            in_specs=[hbm] * 5,
            out_specs=pl.BlockSpec(memory_space=pltpu.VMEM),
            scratch_shapes=[
                pltpu.VMEM((stored, rows, cols), jnp.bfloat16),
                pltpu.VMEM((stored, cols // LANES + 2, rows + 16, LANES), jnp.float32),
                pltpu.VMEM((slices, rows, cols), jnp.int32),
                pltpu.VMEM((rows // part, 2, 8, cols * part // 8), jnp.int32),
                [pltpu.VMEM((bricks, 2, 8, cols * part // 8), jnp.int32)] * blocks,
                pltpu.VMEM((2, slices, cols), jnp.float32),
                pltpu.VMEM((2, slices, cols), jnp.float32),
                pltpu.SemaphoreType.DMA((stored,)),
                pltpu.SemaphoreType.DMA((rows // math.lcm(8, strip),)),
                pltpu.SemaphoreType.DMA((2,)),
                pltpu.SemaphoreType.DMA((2,)),
                pltpu.SemaphoreType.DMA((bricks, blocks)),
                pltpu.SemaphoreType.DMA((bricks, blocks)),
                pltpu.SemaphoreType.DMA((blocks,)),
                pltpu.SMEM((bricks,), jnp.int32),
                pltpu.SMEM(color_table.shape[::-1], jnp.float32),
                pltpu.SMEM(extinction.shape, jnp.float32),
                pltpu.SemaphoreType.DMA((3,)),
            ],
            compiler_params=pltpu.CompilerParams(
                collective_id=0, has_side_effects=True, vmem_limit_bytes=64 * 1024 * 1024
            ),
            cost_estimate=pl.CostEstimate(
                flops=60 * voxels, bytes_accessed=7 * voxels, transcendentals=3 * voxels
            ),
        )(density, material, order, color_table.T, extinction)
        return image.transpose(1, 0, 2)

    placed = (P("depth", "screen", None), P("depth", "screen", None), P(), P(), P())
    return jax.shard_map(
        body,
        mesh=mesh,
        in_specs=placed,
        out_specs=P(None, ("screen", "depth"), None),
        check_vma=False,
    )
```

```python
import functools
import math
import jax
import jax.numpy as jnp
from jax import lax
from jax.experimental import pallas as pl
from jax.experimental.pallas import tpu as pltpu
from jax.sharding import PartitionSpec as P

LIGHT = (0.48, 0.6, 0.64)
MESH = pl.DeviceIdType.MESH
LANES = 128
CODE_TOP = 65000.0
CHUNKS = 4


def kernel(
    bricks, screens, strip,
    dens_hbm, mat_hbm, order_hbm, color_hbm, ext_hbm, out_ref,
    dens, full, mat, sendbuf, recv, halo_out, halo_in,
    dens_sem, mat_sem, halo_send, halo_recv, send_sem, recv_sem, own_sem,
    order_ref, color_ref, ext_ref, small_sem,
):
    stored, rows, cols = dens.shape
    slices = stored - 2
    unit = math.lcm(8, strip)
    units = rows // unit
    groups = unit // 8
    per_unit = unit // strip
    wide = sendbuf.shape[3]
    fold = cols // wide
    part = 8 // fold
    runs = max(1, CHUNKS // fold)
    blocks = strip // part
    entries = ext_ref.shape[0]

    me = lax.axis_index("depth")
    scr = lax.axis_index("screen")
    has_low = scr > 0
    has_high = scr < screens - 1

    own = (me * strip) // unit
    if units == 4:
        across, along = own + 1 - 2 * (own % 2), (own + 2) % 4
        even = me % 2 == 0
        visits = [3 - own, jnp.where(even, across, along), jnp.where(even, along, across), own]
    else:
        visits = [(own + 1 + j) % units for j in range(units)]

    def dens_copy(z):
        return pltpu.make_async_copy(dens_hbm.at[z], dens.at[z], dens_sem.at[z])

    def mat_copy(j):
        where = pl.ds(pl.multiple_of(visits[j] * unit, 8), unit)
        return pltpu.make_async_copy(mat_hbm.at[:, where], mat.at[:, where], mat_sem.at[j])

    small = [
        pltpu.make_async_copy(src, dst, small_sem.at[i])
        for i, (src, dst) in enumerate(
            [(order_hbm, order_ref), (color_hbm, color_ref), (ext_hbm, ext_ref)]
        )
    ]
    for copy in small:
        copy.start()
    for z in range(stored):
        dens_copy(z).start()
    mat_copy(0).start()

    barrier = pltpu.get_barrier_semaphore()
    for peer in range(bricks):
        @pl.when(me != peer)
        def _():
            pl.semaphore_signal(barrier, inc=1, device_id=(peer, scr), device_id_type=MESH)

    @pl.when(has_low)
    def _():
        pl.semaphore_signal(barrier, inc=1, device_id=(me, scr - 1), device_id_type=MESH)

    @pl.when(has_high)
    def _():
        pl.semaphore_signal(barrier, inc=1, device_id=(me, scr + 1), device_id_type=MESH)

    for copy in small:
        copy.wait()

    lane = lax.broadcasted_iota(jnp.int32, (8, LANES), 1)
    sub = lax.broadcasted_iota(jnp.int32, (8, LANES), 0)

    def table(read):
        out = jnp.zeros((8, LANES), jnp.float32)
        for e in range(entries):
            out = jnp.where(lane == e, read(e), out)
        return out

    tabs = [table(lambda e, c=c: color_ref[c, e]) for c in range(3)]
    ext2 = table(lambda e: ext_ref[e]) * math.log2(math.e)
    tops = [jnp.max(t, axis=1, keepdims=True) for t in tabs]
    top_tau = slices * jnp.max(ext2, axis=1, keepdims=True)
    steps = [jnp.broadcast_to(t * (1.0 / CODE_TOP), (8, LANES)) for t in tops + [top_tau]]
    scales = [1.0 / s for s in steps]

    early = 1 if units == 4 and rows == 96 else 0
    upper = visits[0] >= 2

    def convert(z, skip, count):
        @pl.loop(0, count)
        def _(i):
            if skip == 0 and early == 0:
                r = i * 32
            elif skip:
                r = jnp.where(upper, 32, 0) + i * 32
            else:
                r = jnp.where(upper, 0, 64) + i * 32
            r = pl.multiple_of(r, 32)
            full[z, pl.ds(pl.multiple_of(r + 8, 8), 32), LANES : LANES + cols] = dens[
                z, pl.ds(r, 32), :
            ].astype(jnp.float32)

    for z in range(stored):
        dens_copy(z).wait()
        if z == stored - 1:
            for j in range(1, units):
                mat_copy(j).start()
        full[z, 8 : 8 + rows, 0:LANES] = jnp.zeros((rows, LANES), jnp.float32)
        full[z, 8 : 8 + rows, LANES + cols :] = jnp.zeros((rows, LANES), jnp.float32)

        convert(z, 64 * early, rows // 32 - early)
        if 0 < z <= slices:
            halo_out[0, z - 1 : z, :] = dens[z, 0:16, :].astype(jnp.float32)[0:1]
            halo_out[1, z - 1 : z, :] = dens[z, rows - 16 : rows, :].astype(jnp.float32)[15:16]

    pl.semaphore_wait(
        barrier, bricks - 1 + jnp.where(has_low, 1, 0) + jnp.where(has_high, 1, 0)
    )

    def halo_copy(side):
        return pltpu.make_async_remote_copy(
            src_ref=halo_out.at[side],
            dst_ref=halo_in.at[1 - side],
            send_sem=halo_send.at[side],
            recv_sem=halo_recv.at[1 - side],
            device_id=(me, scr + 2 * side - 1),
            device_id_type=MESH,
        )

    def halo_wait(side):
        pltpu.make_async_remote_copy(
            src_ref=halo_out.at[side],
            dst_ref=halo_in.at[side],
            send_sem=halo_send.at[side],
            recv_sem=halo_recv.at[side],
            device_id=(me, scr + 2 * side - 1),
            device_id_type=MESH,
        ).wait_recv()

    @pl.when(has_low)
    def _():
        halo_copy(0).start()

    @pl.when(has_high)
    def _():
        halo_copy(1).start()

    def pixel_tile(r, c):
        def tile(z, dr, dc):
            return full[
                z,
                pl.ds(pl.multiple_of(r + 8 + dr * 8, 8), 8),
                pl.ds(pl.multiple_of(c + (1 + dc) * LANES, LANES), LANES),
            ]

        through = jnp.ones((8, LANES), jnp.float32)
        tau = jnp.zeros((8, LANES), jnp.float32)
        sums = [jnp.zeros((8, LANES), jnp.float32) for _ in range(3)]
        before, here = tile(0, 0, 0), tile(1, 0, 0)
        for z in range(slices):
            after = tile(z + 2, 0, 0)
            left = pltpu.roll(jnp.where(lane == LANES - 1, tile(z + 1, 0, -1), here), 1, 1)
            right = pltpu.roll(jnp.where(lane == 0, tile(z + 1, 0, 1), here), LANES - 1, 1)
            up = pltpu.roll(jnp.where(sub == 7, tile(z + 1, -1, 0), here), 1, 0)
            down = pltpu.roll(jnp.where(sub == 0, tile(z + 1, 1, 0), here), 7, 0)
            dx, dy, dz = right - left, down - up, after - before
            square = (dx * dx + dy * dy) + (dz * dz + 4.0)
            lit = (0.45 * LIGHT[0]) * dx + (0.45 * LIGHT[1]) * dy + (0.45 * LIGHT[2]) * dz
            shade = 0.55 + lit * lax.rsqrt(square)
            kinds = mat[z, pl.ds(r, 8), pl.ds(c, LANES)]

            def pick(values):
                return jnp.take_along_axis(values, kinds, axis=1, mode="promise_in_bounds")

            whole = 1.0 + here
            guess = pl.reciprocal(whole, approx=True)
            sigma = pick(ext2) * (here * (guess * (2.0 - whole * guess)))
            later = through * jnp.exp2(-sigma)
            weight = (through - later) * shade
            for k in range(3):
                sums[k] = sums[k] + weight * pick(tabs[k])
            tau = tau + sigma
            through = later
            before, here = here, after
        gain = 1.0 / (1.0 - through)
        values = [s * gain for s in sums] + [tau]
        codes = [
            jnp.minimum(v * s + 0.5, 65535.0).astype(jnp.int32) for v, s in zip(values, scales)
        ]
        return [(codes[0] << 16) | codes[1], (codes[2] << 16) | codes[3]]

    def row_group(unit_at, g):
        r = pl.multiple_of(unit_at * unit + g * 8, 8)

        @pl.loop(0, wide // (LANES * runs))
        def _(i):
            for k in range(runs):
                c = pl.multiple_of(i * (LANES * runs) + k * LANES, LANES)
                tiles = [pixel_tile(r, pl.multiple_of(f * wide + c, LANES)) for f in range(fold)]
                for h in range(fold):
                    at = unit_at * (unit // part) + g * fold + h
                    for p in range(2):
                        sendbuf[at, p, :, pl.ds(c, LANES)] = jnp.concatenate(
                            [words[p][h * part : (h + 1) * part] for words in tiles], axis=0
                        )

    def strip_copy(s, first=None, count=blocks):
        first = s * blocks if first is None else first
        return pltpu.make_async_remote_copy(
            src_ref=sendbuf.at[pl.ds(first, count)],
            dst_ref=recv.at[me, pl.ds(first - s * blocks, count)],
            send_sem=send_sem.at[s],
            recv_sem=recv_sem.at[me],
            device_id=(s, scr),
            device_id_type=MESH,
        )

    def own_copy(first, count):
        return pltpu.make_async_copy(
            sendbuf.at[pl.ds(first, count)],
            recv.at[me, pl.ds(first - me * blocks, count)],
            own_sem,
        )

    def pieces(group):
        runs = {}
        for b in range(group * (8 // part), (group + 1) * (8 // part)):
            runs.setdefault(b // blocks, []).append(b)
        return [(k, held[0], len(held)) for k, held in runs.items()]

    def send(s, first, count, j):
        if j < units - 1:
            strip_copy(s, first, count).start()
        else:
            @pl.when(s != me)
            def _():
                strip_copy(s, first, count).start()

            @pl.when(s == me)
            def _():
                own_copy(first, count).start()

    def set_halo(side, there):
        row = 7 if side == 0 else 8 + rows

        @pl.when(there)
        def _():
            halo_wait(side)
            for z in range(slices):
                full[z + 1, row : row + 1, LANES : LANES + cols] = halo_in[side, z : z + 1, :]

        @pl.when(jnp.logical_not(there))
        def _():
            for z in range(slices):
                full[z + 1, row : row + 1, LANES : LANES + cols] = jnp.zeros(
                    (1, cols), jnp.float32
                )

    for j in range(units):
        at = visits[j]
        mat_copy(j).wait()
        if j == 1 and early:
            @pl.loop(0, stored)
            def _(z):
                convert(z, 0, 1)

        @pl.loop(0, groups)
        def _(i):
            @pl.when(jnp.logical_and(i == groups - 1, at == 0))
            def _():
                set_halo(0, has_low)

            @pl.when(jnp.logical_and(i == groups - 1, at == units - 1))
            def _():
                set_halo(1, has_high)

            g = jnp.where(at == 0, groups - 1 - i, i)
            row_group(at, g)
            for group in range(groups):
                @pl.when(g == group)
                def _():
                    for k, first, count in pieces(group):
                        send(at * per_unit + k, at * (unit // part) + first, count, j)

    def brick_at(rank):
        def step(j, found):
            return jnp.maximum(found, jnp.where(order_ref[j] == rank, j, 0))

        return lax.fori_loop(0, bricks, step, jnp.int32(0), unroll=bricks <= 8)

    at_rank = [brick_at(i) for i in range(bricks)]

    own_copy(me * blocks, blocks).wait()
    for peer in range(bricks):
        @pl.when(me != peer)
        def _():
            pltpu.make_async_remote_copy(
                src_ref=sendbuf.at[pl.ds(peer * blocks, blocks)],
                dst_ref=recv.at[peer],
                send_sem=send_sem.at[peer],
                recv_sem=recv_sem.at[peer],
                device_id=(peer, scr),
                device_id_type=MESH,
            ).wait_recv()

    width = 2 * LANES
    unscale = [jnp.concatenate([s] * (width // LANES), axis=1) for s in steps]
    for b in range(blocks):
        @pl.loop(0, wide // width)
        def _(i):
            where = pl.ds(pl.multiple_of(i * width, width), width)
            through = jnp.ones((8, width), jnp.float32)
            sums = [jnp.zeros((8, width), jnp.float32) for _ in range(3)]
            for rank in range(bricks):
                first = recv[at_rank[rank], b, 0, :, where]
                second = recv[at_rank[rank], b, 1, :, where]
                codes = []
                for word in (first, second):
                    codes += [lax.shift_right_logical(word, 16), word & 0xFFFF]
                values = [k.astype(jnp.float32) * s for k, s in zip(codes, unscale)]
                later = through * jnp.exp2(-values[3])
                weight = through - later
                sums = [a + weight * v for a, v in zip(sums, values[:3])]
                through = later
            for k, value in enumerate(sums + [1.0 - through]):
                for f in range(fold):
                    to = pl.ds(pl.multiple_of(f * wide + i * width, width), width)
                    for row in range(part):
                        spot = f * part + row
                        out_ref[b * part + row, k : k + 1, to] = value[spot : spot + 1]

    for peer in range(bricks):
        @pl.when(me != peer)
        def _():
            strip_copy(peer).wait_send()

    @pl.when(has_low)
    def _():
        halo_copy(0).wait_send()

    @pl.when(has_high)
    def _():
        halo_copy(1).wait_send()


def solution(mesh):
    bricks, screens = mesh.shape["depth"], mesh.shape["screen"]

    def body(density, material, order, color_table, extinction):
        stored, rows, cols = density.shape
        slices = stored - 2
        strip = rows // bricks
        part = math.gcd(8, strip)
        blocks = strip // part
        hbm = pl.BlockSpec(memory_space=pl.ANY)
        voxels = slices * rows * cols
        image = pl.pallas_call(
            functools.partial(kernel, bricks, screens, strip),
            out_shape=jax.ShapeDtypeStruct((strip, 4, cols), jnp.float32),
            in_specs=[hbm] * 5,
            out_specs=pl.BlockSpec(memory_space=pltpu.VMEM),
            scratch_shapes=[
                pltpu.VMEM((stored, rows, cols), jnp.bfloat16),
                pltpu.VMEM((stored, rows + 16, cols + 2 * LANES), jnp.float32),
                pltpu.VMEM((slices, rows, cols), jnp.int32),
                pltpu.VMEM((rows // part, 2, 8, cols * part // 8), jnp.int32),
                pltpu.VMEM((bricks, blocks, 2, 8, cols * part // 8), jnp.int32),
                pltpu.VMEM((2, slices, cols), jnp.float32),
                pltpu.VMEM((2, slices, cols), jnp.float32),
                pltpu.SemaphoreType.DMA((stored,)),
                pltpu.SemaphoreType.DMA((rows // math.lcm(8, strip),)),
                pltpu.SemaphoreType.DMA((2,)),
                pltpu.SemaphoreType.DMA((2,)),
                pltpu.SemaphoreType.DMA((bricks,)),
                pltpu.SemaphoreType.DMA((bricks,)),
                pltpu.SemaphoreType.DMA,
                pltpu.SMEM((bricks,), jnp.int32),
                pltpu.SMEM(color_table.shape[::-1], jnp.float32),
                pltpu.SMEM(extinction.shape, jnp.float32),
                pltpu.SemaphoreType.DMA((3,)),
            ],
            compiler_params=pltpu.CompilerParams(
                collective_id=0, has_side_effects=True, vmem_limit_bytes=62 * 1024 * 1024
            ),
            cost_estimate=pl.CostEstimate(
                flops=60 * voxels, bytes_accessed=7 * voxels, transcendentals=3 * voxels
            ),
        )(density, material, order, color_table.T, extinction)
        return image.transpose(1, 0, 2)

    placed = (P("depth", "screen", None), P("depth", "screen", None), P(), P(), P())
    return jax.shard_map(
        body,
        mesh=mesh,
        in_specs=placed,
        out_specs=P(None, ("screen", "depth"), None),
        check_vma=False,
    )
```

```python
import functools
import math
import jax
import jax.numpy as jnp
from jax import lax
from jax.experimental import pallas as pl
from jax.experimental.pallas import tpu as pltpu
from jax.sharding import PartitionSpec as P

LIGHT = (0.48, 0.6, 0.64)
MESH = pl.DeviceIdType.MESH
LANES = 128
CODE_TOP = 65000.0
CHUNKS = 8


def kernel(
    bricks, screens, strip,
    dens_hbm, mat_hbm, order_hbm, color_hbm, ext_hbm, out_ref,
    dens, full, mat, sendbuf, recv, halo_out, halo_in,
    dens_sem, mat_sem, halo_send, halo_recv, send_sem, recv_sem, own_sem,
    order_ref, color_ref, ext_ref, small_sem,
):
    stored, rows, cols = dens.shape
    slices = stored - 2
    unit = math.lcm(8, strip)
    units = rows // unit
    groups = unit // 8
    per_unit = unit // strip
    wide = sendbuf.shape[3]
    fold = cols // wide
    part = 8 // fold
    runs = max(1, CHUNKS // fold)
    blocks = strip // part
    entries = ext_ref.shape[0]

    me = lax.axis_index("depth")
    scr = lax.axis_index("screen")
    has_low = scr > 0
    has_high = scr < screens - 1

    own = (me * strip) // unit
    if units == 4:
        across, along = own + 1 - 2 * (own % 2), (own + 2) % 4
        even = me % 2 == 0
        visits = [3 - own, jnp.where(even, across, along), jnp.where(even, along, across), own]
    else:
        visits = [(own + 1 + j) % units for j in range(units)]

    def dens_copy(z):
        return pltpu.make_async_copy(dens_hbm.at[z], dens.at[z], dens_sem.at[z])

    def mat_copy(j):
        where = pl.ds(pl.multiple_of(visits[j] * unit, 8), unit)
        return pltpu.make_async_copy(mat_hbm.at[:, where], mat.at[:, where], mat_sem.at[j])

    small = [
        pltpu.make_async_copy(src, dst, small_sem.at[i])
        for i, (src, dst) in enumerate(
            [(order_hbm, order_ref), (color_hbm, color_ref), (ext_hbm, ext_ref)]
        )
    ]
    for copy in small:
        copy.start()
    for z in range(stored):
        dens_copy(z).start()
    mat_copy(0).start()

    barrier = pltpu.get_barrier_semaphore()
    for peer in range(bricks):
        @pl.when(me != peer)
        def _():
            pl.semaphore_signal(barrier, inc=1, device_id=(peer, scr), device_id_type=MESH)

    @pl.when(has_low)
    def _():
        pl.semaphore_signal(barrier, inc=1, device_id=(me, scr - 1), device_id_type=MESH)

    @pl.when(has_high)
    def _():
        pl.semaphore_signal(barrier, inc=1, device_id=(me, scr + 1), device_id_type=MESH)

    for copy in small:
        copy.wait()

    lane = lax.broadcasted_iota(jnp.int32, (8, LANES), 1)
    sub = lax.broadcasted_iota(jnp.int32, (8, LANES), 0)

    def table(read):
        out = jnp.zeros((8, LANES), jnp.float32)
        for e in range(entries):
            out = jnp.where(lane == e, read(e), out)
        return out

    tabs = [table(lambda e, c=c: color_ref[c, e]) for c in range(3)]
    slope = 0.45 * LIGHT[2]
    ext2 = table(lambda e: ext_ref[e]) * math.log2(math.e)
    tops = [jnp.max(t, axis=1, keepdims=True) for t in tabs]
    top_tau = slices * jnp.max(ext2, axis=1, keepdims=True)
    steps = [jnp.broadcast_to(t * (1.0 / CODE_TOP), (8, LANES)) for t in tops + [top_tau]]
    scales = [1.0 / s for s in steps]
    scales[3] = -scales[3]
    scaled = [t * slope for t in tabs]
    minus_ext2 = -ext2

    early = 1 if units == 4 and rows == 96 else 0
    upper = visits[0] >= 2

    def convert(z, skip, count):
        @pl.loop(0, count)
        def _(i):
            if skip == 0 and early == 0:
                r = i * 32
            elif skip:
                r = jnp.where(upper, 32, 0) + i * 32
            else:
                r = jnp.where(upper, 0, 64) + i * 32
            r = pl.multiple_of(r, 32)
            full[z, pl.ds(pl.multiple_of(r + 8, 8), 32), LANES : LANES + cols] = dens[
                z, pl.ds(r, 32), :
            ].astype(jnp.float32)

    for z in range(stored):
        dens_copy(z).wait()
        if z == stored - 1:
            for j in range(1, units):
                mat_copy(j).start()
        full[z, 8 : 8 + rows, 0:LANES] = jnp.zeros((rows, LANES), jnp.float32)
        full[z, 8 : 8 + rows, LANES + cols :] = jnp.zeros((rows, LANES), jnp.float32)

        convert(z, 64 * early, rows // 32 - early)
        if 0 < z <= slices:
            halo_out[0, z - 1 : z, :] = dens[z, 0:16, :].astype(jnp.float32)[0:1]
            halo_out[1, z - 1 : z, :] = dens[z, rows - 16 : rows, :].astype(jnp.float32)[15:16]

    pl.semaphore_wait(
        barrier, bricks - 1 + jnp.where(has_low, 1, 0) + jnp.where(has_high, 1, 0)
    )

    def halo_copy(side):
        return pltpu.make_async_remote_copy(
            src_ref=halo_out.at[side],
            dst_ref=halo_in.at[1 - side],
            send_sem=halo_send.at[side],
            recv_sem=halo_recv.at[1 - side],
            device_id=(me, scr + 2 * side - 1),
            device_id_type=MESH,
        )

    def halo_wait(side):
        pltpu.make_async_remote_copy(
            src_ref=halo_out.at[side],
            dst_ref=halo_in.at[side],
            send_sem=halo_send.at[side],
            recv_sem=halo_recv.at[side],
            device_id=(me, scr + 2 * side - 1),
            device_id_type=MESH,
        ).wait_recv()

    @pl.when(has_low)
    def _():
        halo_copy(0).start()

    @pl.when(has_high)
    def _():
        halo_copy(1).start()

    def pixel_tile(r, c):
        def tile(z, dr, dc):
            return full[
                z,
                pl.ds(pl.multiple_of(r + 8 + dr * 8, 8), 8),
                pl.ds(pl.multiple_of(c + (1 + dc) * LANES, LANES), LANES),
            ]

        through = jnp.ones((8, LANES), jnp.float32)
        tau = jnp.zeros((8, LANES), jnp.float32)
        sums = [jnp.zeros((8, LANES), jnp.float32) for _ in range(3)]
        before, here = tile(0, 0, 0), tile(1, 0, 0)
        for z in range(slices):
            after = tile(z + 2, 0, 0)
            left = pltpu.roll(jnp.where(lane == LANES - 1, tile(z + 1, 0, -1), here), 1, 1)
            right = pltpu.roll(jnp.where(lane == 0, tile(z + 1, 0, 1), here), LANES - 1, 1)
            up = pltpu.roll(jnp.where(sub == 7, tile(z + 1, -1, 0), here), 1, 0)
            down = pltpu.roll(jnp.where(sub == 0, tile(z + 1, 1, 0), here), 7, 0)
            dx, dy, dz = right - left, down - up, after - before
            square = (dx * dx + dy * dy) + (dz * dz + 4.0)
            lit = (LIGHT[0] / LIGHT[2]) * dx + (LIGHT[1] / LIGHT[2]) * dy + dz
            shade = (0.55 / slope) + lit * lax.rsqrt(square)
            kinds = mat[z, pl.ds(r, 8), pl.ds(c, LANES)]

            def pick(values):
                return jnp.take_along_axis(values, kinds, axis=1, mode="promise_in_bounds")

            whole = 1.0 + here
            guess = pl.reciprocal(whole, approx=True)
            sigma = pick(minus_ext2) * (here * (guess * (2.0 - whole * guess)))
            later = through * jnp.exp2(sigma)
            weight = (through - later) * shade
            for k in range(3):
                sums[k] = sums[k] + weight * pick(scaled[k])
            tau = tau + sigma
            through = later
            before, here = here, after
        dark = 1.0 - through
        gain = pl.reciprocal(dark, approx=True)
        gain = gain * (2.0 - dark * gain)
        values = [s * gain for s in sums] + [tau]
        codes = [(v * s + 0.5).astype(jnp.int32) for v, s in zip(values, scales)]
        return [(codes[0] << 16) | codes[1], (codes[2] << 16) | codes[3]]

    def row_group(unit_at, g):
        r = pl.multiple_of(unit_at * unit + g * 8, 8)

        @pl.loop(0, wide // (LANES * runs))
        def _(i):
            for k in range(runs):
                c = pl.multiple_of(i * (LANES * runs) + k * LANES, LANES)
                tiles = [pixel_tile(r, pl.multiple_of(f * wide + c, LANES)) for f in range(fold)]
                for h in range(fold):
                    at = unit_at * (unit // part) + g * fold + h
                    for p in range(2):
                        sendbuf[at, p, :, pl.ds(c, LANES)] = jnp.concatenate(
                            [words[p][h * part : (h + 1) * part] for words in tiles], axis=0
                        )

    def strip_copy(s, first=None, count=blocks):
        first = s * blocks if first is None else first
        return pltpu.make_async_remote_copy(
            src_ref=sendbuf.at[pl.ds(first, count)],
            dst_ref=recv.at[me, pl.ds(first - s * blocks, count)],
            send_sem=send_sem.at[s],
            recv_sem=recv_sem.at[me],
            device_id=(s, scr),
            device_id_type=MESH,
        )

    def own_copy(first, count):
        return pltpu.make_async_copy(
            sendbuf.at[pl.ds(first, count)],
            recv.at[me, pl.ds(first - me * blocks, count)],
            own_sem,
        )

    def pieces(group):
        runs = {}
        for b in range(group * (8 // part), (group + 1) * (8 // part)):
            runs.setdefault(b // blocks, []).append(b)
        return [(k, held[0], len(held)) for k, held in runs.items()]

    def send(s, first, count, j):
        if j < units - 1:
            strip_copy(s, first, count).start()
        else:
            @pl.when(s != me)
            def _():
                strip_copy(s, first, count).start()

            @pl.when(s == me)
            def _():
                own_copy(first, count).start()

    def set_halo(side, there):
        row = 7 if side == 0 else 8 + rows

        @pl.when(there)
        def _():
            halo_wait(side)
            for z in range(slices):
                full[z + 1, row : row + 1, LANES : LANES + cols] = halo_in[side, z : z + 1, :]

        @pl.when(jnp.logical_not(there))
        def _():
            for z in range(slices):
                full[z + 1, row : row + 1, LANES : LANES + cols] = jnp.zeros(
                    (1, cols), jnp.float32
                )

    for j in range(units):
        at = visits[j]
        mat_copy(j).wait()
        if j == 1 and early:
            @pl.loop(0, stored)
            def _(z):
                convert(z, 0, 1)

        @pl.loop(0, groups)
        def _(i):
            @pl.when(jnp.logical_and(i == groups - 1, at == 0))
            def _():
                set_halo(0, has_low)

            @pl.when(jnp.logical_and(i == groups - 1, at == units - 1))
            def _():
                set_halo(1, has_high)

            g = jnp.where(at == 0, groups - 1 - i, i)
            row_group(at, g)
            for group in range(groups):
                @pl.when(g == group)
                def _():
                    for k, first, count in pieces(group):
                        send(at * per_unit + k, at * (unit // part) + first, count, j)

    def brick_at(rank):
        def step(j, found):
            return jnp.maximum(found, jnp.where(order_ref[j] == rank, j, 0))

        return lax.fori_loop(0, bricks, step, jnp.int32(0), unroll=bricks <= 8)

    at_rank = [brick_at(i) for i in range(bricks)]

    own_copy(me * blocks, blocks).wait()
    for peer in range(bricks):
        @pl.when(me != peer)
        def _():
            pltpu.make_async_remote_copy(
                src_ref=sendbuf.at[pl.ds(peer * blocks, blocks)],
                dst_ref=recv.at[peer],
                send_sem=send_sem.at[peer],
                recv_sem=recv_sem.at[peer],
                device_id=(peer, scr),
                device_id_type=MESH,
            ).wait_recv()

    width = 2 * LANES
    unscale = [jnp.concatenate([s] * (width // LANES), axis=1) for s in steps]
    for b in range(blocks):
        @pl.loop(0, wide // width)
        def _(i):
            where = pl.ds(pl.multiple_of(i * width, width), width)
            through = jnp.ones((8, width), jnp.float32)
            sums = [jnp.zeros((8, width), jnp.float32) for _ in range(3)]
            for rank in range(bricks):
                first = recv[at_rank[rank], b, 0, :, where]
                second = recv[at_rank[rank], b, 1, :, where]
                codes = []
                for word in (first, second):
                    codes += [lax.shift_right_logical(word, 16), word & 0xFFFF]
                values = [k.astype(jnp.float32) * s for k, s in zip(codes, unscale)]
                later = through * jnp.exp2(-values[3])
                weight = through - later
                sums = [a + weight * v for a, v in zip(sums, values[:3])]
                through = later
            for k, value in enumerate(sums + [1.0 - through]):
                for f in range(fold):
                    to = pl.ds(pl.multiple_of(f * wide + i * width, width), width)
                    for row in range(part):
                        spot = f * part + row
                        out_ref[b * part + row, k : k + 1, to] = value[spot : spot + 1]

    for peer in range(bricks):
        @pl.when(me != peer)
        def _():
            strip_copy(peer).wait_send()

    @pl.when(has_low)
    def _():
        halo_copy(0).wait_send()

    @pl.when(has_high)
    def _():
        halo_copy(1).wait_send()


def solution(mesh):
    bricks, screens = mesh.shape["depth"], mesh.shape["screen"]

    def body(density, material, order, color_table, extinction):
        stored, rows, cols = density.shape
        slices = stored - 2
        strip = rows // bricks
        part = math.gcd(8, strip)
        blocks = strip // part
        hbm = pl.BlockSpec(memory_space=pl.ANY)
        voxels = slices * rows * cols
        image = pl.pallas_call(
            functools.partial(kernel, bricks, screens, strip),
            out_shape=jax.ShapeDtypeStruct((strip, 4, cols), jnp.float32),
            in_specs=[hbm] * 5,
            out_specs=pl.BlockSpec(memory_space=pltpu.VMEM),
            scratch_shapes=[
                pltpu.VMEM((stored, rows, cols), jnp.bfloat16),
                pltpu.VMEM((stored, rows + 16, cols + 2 * LANES), jnp.float32),
                pltpu.VMEM((slices, rows, cols), jnp.int32),
                pltpu.VMEM((rows // part, 2, 8, cols * part // 8), jnp.int32),
                pltpu.VMEM((bricks, blocks, 2, 8, cols * part // 8), jnp.int32),
                pltpu.VMEM((2, slices, cols), jnp.float32),
                pltpu.VMEM((2, slices, cols), jnp.float32),
                pltpu.SemaphoreType.DMA((stored,)),
                pltpu.SemaphoreType.DMA((rows // math.lcm(8, strip),)),
                pltpu.SemaphoreType.DMA((2,)),
                pltpu.SemaphoreType.DMA((2,)),
                pltpu.SemaphoreType.DMA((bricks,)),
                pltpu.SemaphoreType.DMA((bricks,)),
                pltpu.SemaphoreType.DMA,
                pltpu.SMEM((bricks,), jnp.int32),
                pltpu.SMEM(color_table.shape[::-1], jnp.float32),
                pltpu.SMEM(extinction.shape, jnp.float32),
                pltpu.SemaphoreType.DMA((3,)),
            ],
            compiler_params=pltpu.CompilerParams(
                collective_id=0, has_side_effects=True, vmem_limit_bytes=62 * 1024 * 1024
            ),
            cost_estimate=pl.CostEstimate(
                flops=60 * voxels, bytes_accessed=7 * voxels, transcendentals=3 * voxels
            ),
        )(density, material, order, color_table.T, extinction)
        return image.transpose(1, 0, 2)

    placed = (P("depth", "screen", None), P("depth", "screen", None), P(), P(), P())
    return jax.shard_map(
        body,
        mesh=mesh,
        in_specs=placed,
        out_specs=P(None, ("screen", "depth"), None),
        check_vma=False,
    )
```
